128 devices in a mesh: gx: 8 (over z_hi, x), gy: 16 (over y, z_lo, core).
Axes of the slice: x: 4, y: 4, z: 4 (z_hi: 2, z_lo: 2; z = z_hi * 2 + z_lo), core: 2. Of those that a mesh axis runs over, the one named last changes fastest.
Arguments:
- latent: bfloat16 [256, 1024, 512], P('gx', 'gy'), may hold values from -6 to 6
- cotangent: bfloat16 [256, 1024, 512], P('gx', 'gy'), may hold values from -6 to 6
- layer_norm_gain: float32 [512], replicated, may hold values from 0.1 to 1.9
- layer_norm_bias: float32 [512], replicated, may hold values from -3 to 3
- w_qkv: bfloat16 [512, 1536], replicated, may hold values from -0.25 to 0.25
- w_out: bfloat16 [512, 512], replicated, may hold values from -0.25 to 0.25
- rel_bias: float32 [16, 225], replicated, may hold values from -2 to 250
Outputs:
- latent_gradient: bfloat16 [256, 1024, 512], P('gx', 'gy')
- d_w_qkv: float32 [512, 1536], replicated
- d_w_out: float32 [512, 512], replicated
- d_ln_gain: float32 [512], replicated
- d_ln_bias: float32 [512], replicated
The draws below stay inside these ranges and needn't reach their ends.
All inputs are finite; a program needn't handle non-finite values.
Results may differ from the reference program's by a relative error of at most 0.0097.
Values may be sent and summed in bfloat16 or wider, within the bound.
No kernel may reach another device: no remote copies, remote signals or barrier semaphores. Data moves between devices by JAX's collectives and lax.ppermute only.
A program may use at most 192 MiB of HBM per device.

```python
import math
import jax
import jax.numpy as jnp
from jax import lax

C = 512
HEADS = 16
H = 256
W = 1024


def draw_rel_bias(key, part):
    key = jax.random.fold_in(key, 7)
    key_base = jax.random.fold_in(key, 0)
    base = jax.random.uniform(key_base, (HEADS, 225), jnp.float32, -2.0, 2.0)
    return base


def block_scale(stream_key, extent, cuts, low, top_value):
    gain = 1.0
    for dim, parts in cuts:
        heights = jax.random.uniform(jax.random.fold_in(jax.random.fold_in(stream_key, 6), dim), (parts,), jnp.float32, low / len(cuts), top_value / len(cuts))
        gain = gain * jnp.repeat(jnp.exp(heights), extent[dim] // parts).reshape((-1,) + (1,) * (len(extent) - 1 - dim))
    return gain


def centred(key, shape, scale, reach, pieces=(), held_as=jnp.bfloat16):
    values = scale * jax.random.normal(key, shape, jnp.float32)
    if pieces:
        values = values * block_scale(key, shape, pieces, -0.22, 0.18)
    return jnp.clip(values, -reach, reach).astype(held_as)


def setup_inputs(seed: int = 0) -> dict:
    arg_keys = jax.random.split(jax.random.key(seed), 8)
    latent = centred(arg_keys[0], (H, W, C), 1.0, 6.0, ((0, 8), (1, 16)))
    cotangent = centred(arg_keys[1], (H, W, C), 1.0, 6.0, ((0, 8), (1, 16)))
    layer_norm_gain = jnp.clip(1.0 + 0.18 * jax.random.normal(arg_keys[2], (C,), jnp.float32), 0.1, 1.9)
    layer_norm_bias = centred(arg_keys[3], (C,), 0.5, 3.0, (), jnp.float32)
    w_qkv = centred(arg_keys[4], (C, 3 * C), C ** -0.5, 0.25)
    w_out = centred(arg_keys[5], (C, C), C ** -0.5, 0.25)
    rel_bias = draw_rel_bias(jax.random.fold_in(arg_keys[7], 71), 0)
    return dict(latent=latent, cotangent=cotangent, layer_norm_gain=layer_norm_gain, layer_norm_bias=layer_norm_bias, w_qkv=w_qkv, w_out=w_out, rel_bias=rel_bias)


def bias_table(rel_bias):
    position = jnp.arange(64, dtype=jnp.int32)
    prow = position // 8
    pcol = position % 8
    offset = (prow[:, None] - prow[None, :] + 7) * 15 + (pcol[:, None] - pcol[None, :] + 7)
    onehot = (offset.reshape(1, 4096) == jnp.arange(225, dtype=jnp.int32)[:, None]).astype(jnp.float32)
    full = jnp.dot(rel_bias, onehot, precision=lax.Precision.HIGHEST)
    return full.reshape(rel_bias.shape[0], 64, 64)

def window_backward(latent_w, weight_cotangent, layer_norm_gain, layer_norm_bias, w_qkv, w_out, bias_full):
    count, width = (latent_w.shape[0], latent_w.shape[2])
    heads = bias_full.shape[0]
    head_dim = width // heads
    factor = 1.0 / math.sqrt(head_dim)
    values = latent_w.astype(jnp.float32)
    centre = lax.optimization_barrier(jnp.mean(values, -1, keepdims=True))
    centred_latent = values - centre
    variance = lax.optimization_barrier(jnp.mean(centred_latent * centred_latent, -1, keepdims=True))
    inverse_deviation = lax.rsqrt(variance + 1e-05)
    standardised_latent = centred_latent * inverse_deviation
    normed_latent = (standardised_latent * layer_norm_gain + layer_norm_bias).astype(jnp.bfloat16)
    flat_normed = normed_latent.reshape(-1, width)
    qkv = jnp.dot(flat_normed, w_qkv, preferred_element_type=jnp.float32).astype(jnp.bfloat16)
    qkv = qkv.reshape(count, 64, 3, heads, head_dim)
    query = qkv[:, :, 0].astype(jnp.float32)
    keys = qkv[:, :, 1].astype(jnp.float32)
    vals = qkv[:, :, 2].astype(jnp.float32)
    scores = jnp.einsum('wqhd,wkhd->whqk', query, keys) * factor + bias_full[None]
    highest = lax.optimization_barrier(jnp.max(scores, -1, keepdims=True))
    probs = jnp.exp(scores - highest)
    probs = probs / lax.optimization_barrier(jnp.sum(probs, -1, keepdims=True))
    probs_b = probs.astype(jnp.bfloat16).astype(jnp.float32)
    attended = jnp.einsum('whqk,wkhd->wqhd', probs_b, vals).astype(jnp.bfloat16).reshape(-1, width)
    cot_flat = weight_cotangent.reshape(-1, width)
    grad_out = jnp.dot(attended.T, cot_flat, preferred_element_type=jnp.float32)
    d_att = jnp.dot(cot_flat, w_out.T, preferred_element_type=jnp.float32).astype(jnp.bfloat16)
    d_att = d_att.reshape(count, 64, heads, head_dim).astype(jnp.float32)
    d_probs = jnp.einsum('wqhd,wkhd->whqk', d_att, vals)
    d_vals = jnp.einsum('whqk,wqhd->wkhd', probs_b, d_att)
    d_scores = probs * (d_probs - lax.optimization_barrier(jnp.sum(probs * d_probs, -1, keepdims=True)))
    ds_b = d_scores.astype(jnp.bfloat16).astype(jnp.float32)
    d_query = jnp.einsum('whqk,wkhd->wqhd', ds_b, keys) * factor
    d_keys = jnp.einsum('whqk,wqhd->wkhd', ds_b, query) * factor
    d_qkv = jnp.stack([d_query, d_keys, d_vals], axis=2).astype(jnp.bfloat16).reshape(-1, 3 * width)
    grad_qkv = jnp.dot(flat_normed.T, d_qkv, preferred_element_type=jnp.float32)
    normed_gradient = jnp.dot(d_qkv, w_qkv.T, preferred_element_type=jnp.float32).reshape(count, 64, width)
    gain_gradient = lax.optimization_barrier(jnp.sum(standardised_latent * normed_gradient, axis=(0, 1)))
    grad_bias = lax.optimization_barrier(jnp.sum(normed_gradient, axis=(0, 1)))
    normalised_gradient = normed_gradient * layer_norm_gain
    latent_gradient = weight_cotangent.astype(jnp.float32) + inverse_deviation * (normalised_gradient - lax.optimization_barrier(jnp.mean(normalised_gradient, -1, keepdims=True)) - standardised_latent * lax.optimization_barrier(jnp.mean(normalised_gradient * standardised_latent, -1, keepdims=True)))
    return (latent_gradient.astype(jnp.bfloat16), grad_qkv, grad_out, gain_gradient, grad_bias)

def reference(latent, cotangent, layer_norm_gain, layer_norm_bias, w_qkv, w_out, rel_bias):
    rows_all, cols_all, width = latent.shape
    stride_r = rows_all // 8
    stride_c = cols_all // 8

    def to_windows(array):
        return array.reshape(8, stride_r, 8, stride_c, width).transpose(1, 3, 0, 2, 4).reshape(-1, 64, width)
    latent_w = to_windows(latent)
    weight_cotangent = to_windows(cotangent)
    total = latent_w.shape[0]
    group = math.gcd(total, 64)
    blocks = total // group
    bias_full = bias_table(rel_bias)

    def step(carry, item):
        latent_b, cot_b = item
        d_block, grad_qkv, grad_out, gain_gradient, grad_bias = window_backward(latent_b, cot_b, layer_norm_gain, layer_norm_bias, w_qkv, w_out, bias_full)
        return ((carry[0] + grad_qkv, carry[1] + grad_out, carry[2] + gain_gradient, carry[3] + grad_bias), d_block)
    init = (jnp.zeros((width, 3 * width), jnp.float32), jnp.zeros((width, width), jnp.float32), jnp.zeros((width,), jnp.float32), jnp.zeros((width,), jnp.float32))
    sums, d_blocks = lax.scan(step, init, (latent_w.reshape(blocks, group, 64, width), weight_cotangent.reshape(blocks, group, 64, width)))
    latent_gradient = d_blocks.reshape(stride_r, stride_c, 8, 8, width).transpose(2, 0, 3, 1, 4).reshape(rows_all, cols_all, width)
    norm = 1.0 / math.sqrt(rows_all * cols_all)
    return (latent_gradient, sums[0] * norm, sums[1] * norm, sums[2] * norm, sums[3] * norm)
```

```python
import math

import jax
import jax.numpy as jnp
from jax import lax
from jax.experimental import pallas as pl
from jax.experimental.pallas import tpu as pltpu
from jax.sharding import Mesh, PartitionSpec as P

F32 = jnp.float32
BF16 = jnp.bfloat16
HEADS = 16
CELLS = 64
PARTS = 2
STEP = 4
ROWS = STEP * CELLS
GROUPS = 4
FACTOR = 1.0 / math.sqrt(32.0)
NATURAL = (0, 1, 2, 3)
SWAPPED = (0, 2, 1, 3)
MIB = 1 << 20


def dot(left, right):
    return jnp.dot(left, right, preferred_element_type=F32)


def dot_cols(left, right):
    return lax.dot_general(left, right, (((1,), (1,)), ((), ())), preferred_element_type=F32)


def dot_rows(left, right):
    return lax.dot_general(left, right, (((0,), (0,)), ((), ())), preferred_element_type=F32)


def spread(block, mask_ref, order):
    return jnp.concatenate([block * mask_ref[h] for h in order], axis=0)


def turn(block):
    tall = jnp.concatenate([block[:, :128], block[:, 128:]], axis=0)
    tall = tall.T
    return jnp.concatenate([tall[:64], tall[64:]], axis=1)


def scatter_rows(source_ref, slab):
    windows = source_ref.shape[1]

    def fill(n, carry):
        rows = pl.ds(pl.multiple_of(n * windows, windows), windows)
        for k in range(4):
            slab[k, rows, :] = source_ref[n, :, k * 128 : k * 128 + 128].astype(F32)
        return carry

    lax.fori_loop(0, CELLS, fill, 0)


def window_rows(slab, first, windows):
    return jnp.concatenate(
        [
            jnp.concatenate(
                [slab[k, pl.ds(first + j, CELLS, stride=windows), :] for j in range(STEP)], axis=0
            )
            for k in range(4)
        ],
        axis=1,
    )


def standardise(values):
    centred = values - jnp.mean(values, -1, keepdims=True)
    variance = jnp.mean(centred * centred, -1, keepdims=True)
    inverse = lax.rsqrt(variance + 1e-05)
    return centred * inverse, inverse


def forward_kernel(
    x_ref, gain_ref, shift_ref, wqkv_ref, bias_ref, mask_ref,
    xw_ref, qkv_ref, probs_ref, att_ref, slab
):
    windows = x_ref.shape[1]
    step = pl.program_id(0)

    @pl.when(step == 0)
    def _():
        scatter_rows(x_ref, slab)

    values = window_rows(slab, step * STEP, windows)
    xw_ref[...] = values.astype(BF16)
    xhat, _ = standardise(values)
    normed = (xhat * gain_ref[...] + shift_ref[...]).astype(BF16)
    qkv_ref[...] = dot(normed, wqkv_ref[...]).astype(BF16)
    for j in range(STEP):
        rows = pl.ds(j * CELLS, CELLS)
        for g in range(GROUPS):
            q4 = qkv_ref[rows, g * 128 : g * 128 + 128]
            k4 = qkv_ref[rows, 512 + g * 128 : 512 + g * 128 + 128]
            v4 = qkv_ref[rows, 1024 + g * 128 : 1024 + g * 128 + 128]
            scores = dot_cols(k4, spread(q4, mask_ref, NATURAL)) * FACTOR + bias_ref[g]
            probs = jnp.exp(scores - jnp.max(scores, 0, keepdims=True))
            probs = probs * (1.0 / jnp.sum(probs, 0, keepdims=True))
            probs = probs.astype(BF16)
            probs_ref[pl.ds((j * GROUPS + g) * CELLS, CELLS), :] = probs
            att_ref[rows, g * 128 : g * 128 + 128] = dot(
                turn(probs), spread(v4, mask_ref, SWAPPED)
            ).astype(BF16)


def backward_kernel(
    cot_ref, xw_ref, qkv_ref, probs_ref, att_ref, gain_ref, shift_ref, wqkv_ref, wout_ref, mask_ref,
    *refs, first
):
    if first:
        out_ref, gq_ref, go_ref, ln_ref, slab, result, dqkv = refs
    else:
        gq_in, go_in, ln_in, out_ref, gq_ref, go_ref, ln_ref, slab, result, dqkv = refs
    windows = cot_ref.shape[1]
    step = pl.program_id(0)

    @pl.when(step == 0)
    def _():
        scatter_rows(cot_ref, slab)
        if first:
            gq_ref[...] = jnp.zeros_like(gq_ref)
            go_ref[...] = jnp.zeros_like(go_ref)
            ln_ref[...] = jnp.zeros_like(ln_ref)
        else:
            gq_ref[...] = gq_in[...]
            go_ref[...] = go_in[...]
            ln_ref[...] = ln_in[...]

    cot = window_rows(slab, step * STEP, windows)
    cot_b = cot.astype(BF16)
    d_att = dot_cols(cot_b, wout_ref[...]).astype(BF16)
    for j in range(STEP):
        rows = pl.ds(j * CELLS, CELLS)
        for g in range(GROUPS):
            lanes = slice(g * 128, g * 128 + 128)
            q4 = qkv_ref[rows, g * 128 : g * 128 + 128]
            k4 = qkv_ref[rows, 512 + g * 128 : 512 + g * 128 + 128]
            v4 = qkv_ref[rows, 1024 + g * 128 : 1024 + g * 128 + 128]
            d_att_bd = spread(d_att[j * CELLS : j * CELLS + CELLS, lanes], mask_ref, NATURAL)
            probs_b = probs_ref[pl.ds((j * GROUPS + g) * CELLS, CELLS), :]
            probs = probs_b.astype(F32)
            d_probs = dot_cols(v4, d_att_bd)
            d_scores = probs * (d_probs - jnp.sum(probs * d_probs, 0, keepdims=True))
            ds_b = d_scores.astype(BF16)
            d_vals = dot(probs_b, d_att_bd)
            d_keys = dot(ds_b, spread(q4, mask_ref, NATURAL)) * FACTOR
            d_query = dot(turn(ds_b), spread(k4, mask_ref, SWAPPED)) * FACTOR
            dqkv[rows, g * 128 : g * 128 + 128] = d_query.astype(BF16)
            dqkv[rows, 512 + g * 128 : 512 + g * 128 + 128] = d_keys.astype(BF16)
            dqkv[rows, 1024 + g * 128 : 1024 + g * 128 + 128] = d_vals.astype(BF16)
    go_ref[...] += dot_rows(att_ref[...], cot_b)
    xhat, inverse = standardise(xw_ref[...].astype(F32))
    normed = (xhat * gain_ref[...] + shift_ref[...]).astype(BF16)
    d_qkv = dqkv[...]
    gq_ref[...] += dot_rows(normed, d_qkv)
    d_normed = dot_cols(d_qkv, wqkv_ref[...])
    weighted = xhat * d_normed
    ln_ref[0] += jnp.sum(weighted.reshape(ROWS // 8, 8, 512), 0)
    ln_ref[1] += jnp.sum(d_normed.reshape(ROWS // 8, 8, 512), 0)
    d_hat = d_normed * gain_ref[...]
    value = cot + inverse * (
        d_hat
        - jnp.mean(d_hat, -1, keepdims=True)
        - xhat * jnp.mean(d_hat * xhat, -1, keepdims=True)
    )
    for j in range(STEP):
        for k in range(4):
            result[k, pl.ds(step * STEP + j, CELLS, stride=windows), :] = value[
                j * CELLS : j * CELLS + CELLS, k * 128 : k * 128 + 128
            ]

    @pl.when(step == pl.num_programs(0) - 1)
    def _():
        def empty(n, carry):
            rows = pl.ds(pl.multiple_of(n * windows, windows), windows)
            for k in range(4):
                out_ref[n, :, k * 128 : k * 128 + 128] = result[k, rows, :].astype(BF16)
            return carry

        lax.fori_loop(0, CELLS, empty, 0)


def whole(shape):
    return pl.BlockSpec(shape, lambda i: (0,) * len(shape))


def rows_spec(rows, width, offset=0):
    return pl.BlockSpec((rows, width), lambda i: (i + offset, 0))


def forward(x, gain, shift, w_qkv, bias, mask):
    windows = x.shape[1]
    cells = windows * CELLS
    return pl.pallas_call(
        forward_kernel,
        grid=(windows // STEP,),
        in_specs=[
            whole(x.shape), whole(gain.shape), whole(shift.shape), whole(w_qkv.shape),
            whole(bias.shape), whole(mask.shape),
        ],
        out_specs=[
            rows_spec(ROWS, 512), rows_spec(ROWS, 1536),
            rows_spec(ROWS * GROUPS, 256), rows_spec(ROWS, 512),
        ],
        out_shape=[
            jax.ShapeDtypeStruct((cells, 512), BF16),
            jax.ShapeDtypeStruct((cells, 1536), BF16),
            jax.ShapeDtypeStruct((cells * GROUPS, 256), BF16),
            jax.ShapeDtypeStruct((cells, 512), BF16),
        ],
        scratch_shapes=[pltpu.VMEM((4, cells, 128), F32)],
        compiler_params=pltpu.CompilerParams(vmem_limit_bytes=40 * MIB),
        cost_estimate=pl.CostEstimate(
            flops=15 * 10**9, bytes_accessed=20 * MIB, transcendentals=2 * 10**6
        ),
        name="window_forward",
    )(x, gain, shift, w_qkv, bias, mask)


def backward(part, cot, saved, gain, shift, w_qkv, w_out, mask, sums):
    windows = cot.shape[1]
    steps = windows // STEP
    xw, qkv, probs, att = saved
    off = part * steps
    grads = [
        jax.ShapeDtypeStruct((512, 1536), F32),
        jax.ShapeDtypeStruct((512, 512), F32),
        jax.ShapeDtypeStruct((2, 8, 512), F32),
    ]

    def kernel(*refs):
        backward_kernel(*refs, first=sums is None)

    return pl.pallas_call(
        kernel,
        grid=(steps,),
        in_specs=[
            whole(cot.shape),
            rows_spec(ROWS, 512, off), rows_spec(ROWS, 1536, off),
            rows_spec(ROWS * GROUPS, 256, off), rows_spec(ROWS, 512, off),
            whole(gain.shape), whole(shift.shape), whole(w_qkv.shape), whole(w_out.shape),
            whole(mask.shape),
        ]
        + ([] if sums is None else [whole(s.shape) for s in sums]),
        out_specs=[whole(cot.shape)] + [whole(s.shape) for s in grads],
        out_shape=[jax.ShapeDtypeStruct(cot.shape, BF16)] + grads,
        scratch_shapes=[
            pltpu.VMEM((4, windows * CELLS, 128), F32),
            pltpu.VMEM((4, windows * CELLS, 128), F32),
            pltpu.VMEM((ROWS, 1536), BF16),
        ],
        compiler_params=pltpu.CompilerParams(vmem_limit_bytes=48 * MIB),
        cost_estimate=pl.CostEstimate(
            flops=15 * 10**9, bytes_accessed=20 * MIB, transcendentals=0
        ),
        name="window_backward",
    )(cot, xw, qkv, probs, att, gain, shift, w_qkv, w_out, mask, *(sums or ()))


def bias_tables(rel_bias):
    position = jnp.arange(CELLS, dtype=jnp.int32)
    prow = position // 8
    pcol = position % 8
    offset = (prow[None, :] - prow[:, None] + 7) * 15 + (pcol[None, :] - pcol[:, None] + 7)
    onehot = (offset.reshape(1, -1) == jnp.arange(225, dtype=jnp.int32)[:, None]).astype(F32)
    full = jnp.dot(rel_bias, onehot, precision=lax.Precision.HIGHEST)
    full = full.reshape(GROUPS, HEADS // GROUPS, CELLS, CELLS).transpose(0, 2, 1, 3)
    return full.reshape(GROUPS, CELLS, 256)


def after(value, *others):
    return lax.optimization_barrier((value,) + others)[0]


def exchange(array):
    return lax.all_to_all(array, ("gx", "gh"), split_axis=0, concat_axis=0, tiled=True)


def swap_cores(array):
    return lax.ppermute(array, "core", [(0, 1), (1, 0)])


def body(latent, cotangent, gain, shift, w_qkv, w_out, rel_bias):
    rows, cols, width = latent.shape
    peers = lax.axis_size("gx") * lax.axis_size("gh")
    windows = rows * cols // peers
    per_part = windows // PARTS
    norm = 1.0 / math.sqrt(rows * cols * peers * lax.axis_size("core"))
    core = lax.axis_index("core")
    gain = gain.reshape(1, width)
    shift = shift.reshape(1, width)
    lane = jnp.arange(128, dtype=jnp.int32) // 32
    mask = jnp.broadcast_to(
        (lane[None, None, :] == jnp.arange(4, dtype=jnp.int32)[:, None, None]).astype(BF16),
        (4, CELLS, 128),
    )
    bias = bias_tables(rel_bias)

    latent = latent.reshape(peers, windows, width)
    cotangent = cotangent.reshape(peers, windows, width)
    x = exchange(latent)
    previous = x
    cots = []
    for p in range(PARTS):
        piece = after(cotangent[:, p * per_part : (p + 1) * per_part], previous)
        previous = exchange(piece)
        cots.append(previous)
    saved = forward(x, gain, shift, w_qkv, bias, mask)
    sums = None
    pieces = []
    for p in range(PARTS):
        d_latent, *sums = backward(p, cots[p], saved, gain, shift, w_qkv, w_out, mask, sums)
        pieces.append(exchange(d_latent))
    grad_qkv, grad_out, ln = sums
    result = jnp.concatenate(pieces, axis=1).reshape(rows, cols, width)

    ln = jnp.sum(ln, axis=1)
    column = jnp.zeros((2, width, 128), F32).at[:, :, 0].set(ln)
    halves = jnp.stack(
        [
            jnp.concatenate([grad_qkv[:, :1024], column[0]], axis=1),
            jnp.concatenate([grad_qkv[:, 1024:], grad_out, column[1]], axis=1),
        ]
    )
    mine = lax.dynamic_index_in_dim(halves, core, 0, keepdims=False)
    other = lax.dynamic_index_in_dim(halves, 1 - core, 0, keepdims=False).astype(BF16)
    mine = (mine + swap_cores(other).astype(F32)).astype(BF16)
    parts = exchange(mine.reshape(peers, 8, 1152))
    total = (jnp.sum(parts.astype(F32), axis=0) * norm).astype(BF16)
    full = exchange(jnp.broadcast_to(total[None], parts.shape)).reshape(width, 1152)
    theirs = swap_cores(full)
    low = jnp.where(core == 0, full, theirs).astype(F32)
    high = jnp.where(core == 0, theirs, full).astype(F32)
    return (
        result,
        jnp.concatenate([low[:, :1024], high[:, :512]], axis=1),
        high[:, 512:1024],
        low[:, 1024],
        high[:, 1024],
    )


def solution(mesh):
    cores = mesh.devices.reshape(mesh.shape["gx"], mesh.shape["gy"] // 2, 2)
    inner = Mesh(cores, ("gx", "gh", "core"))
    block = P("gx", ("gh", "core"), None)
    return jax.shard_map(
        body,
        mesh=inner,
        in_specs=(block, block, P(), P(), P(), P(), P()),
        out_specs=(block, P(), P(), P(), P()),
        check_vma=False,
    )
```

```python
import math

import jax
import jax.numpy as jnp
from jax import lax
from jax.experimental import pallas as pl
from jax.experimental.pallas import tpu as pltpu
from jax.sharding import Mesh, PartitionSpec as P

F32 = jnp.float32
BF16 = jnp.bfloat16
HEADS = 16
CELLS = 64
PARTS = 2
STEP = 4
ROWS = STEP * CELLS
GROUPS = 4
FACTOR = 1.0 / math.sqrt(32.0)
NATURAL = (0, 1, 2, 3)
SWAPPED = (0, 2, 1, 3)
SKEW = 1
MIB = 1 << 20


def dot(left, right):
    return jnp.dot(left, right, preferred_element_type=F32)


def dot_cols(left, right):
    return lax.dot_general(left, right, (((1,), (1,)), ((), ())), preferred_element_type=F32)


def dot_rows(left, right):
    return lax.dot_general(left, right, (((0,), (0,)), ((), ())), preferred_element_type=F32)


def spread(block, mask_ref, order):
    return jnp.concatenate([block * mask_ref[h] for h in order], axis=0)


def turn(block):
    tall = jnp.concatenate([block[:, :128], block[:, 128:]], axis=0)
    tall = tall.T
    return jnp.concatenate([tall[:64], tall[64:]], axis=1)


def window_rows(slab, first, windows):
    return jnp.concatenate(
        [
            jnp.concatenate(
                [slab[k, pl.ds(first + j, CELLS, stride=windows), :] for j in range(STEP)], axis=0
            )
            for k in range(4)
        ],
        axis=1,
    )


def standardise(values):
    centred = values - jnp.mean(values, -1, keepdims=True)
    variance = jnp.mean(centred * centred, -1, keepdims=True)
    inverse = lax.rsqrt(variance + 1e-05)
    return centred * inverse, inverse


def unit(j, g, qkv, d_att, d_qkv, att, bias_ref, mask_ref):
    rows = pl.ds(j * CELLS, CELLS)
    lane = g * 128
    q4 = qkv[rows, lane : lane + 128]
    k4 = qkv[rows, 512 + lane : 512 + lane + 128]
    v4 = qkv[rows, 1024 + lane : 1024 + lane + 128]
    q_wide = spread(q4, mask_ref, NATURAL)
    d_att_wide = spread(d_att[rows, lane : lane + 128], mask_ref, NATURAL)
    scores = dot_cols(k4, q_wide) * FACTOR + bias_ref[g]
    d_probs = dot_cols(v4, d_att_wide)
    yield
    probs = jnp.exp(scores - jnp.max(scores, 0, keepdims=True))
    probs = probs * (1.0 / jnp.sum(probs, 0, keepdims=True))
    probs_b = probs.astype(BF16)
    d_scores = probs * (d_probs - jnp.sum(probs * d_probs, 0, keepdims=True))
    ds_b = d_scores.astype(BF16)
    yield
    turned = turn(probs_b)
    ds_turned = turn(ds_b)
    yield
    attended = dot(turned, spread(v4, mask_ref, SWAPPED))
    d_query = dot(ds_turned, spread(k4, mask_ref, SWAPPED)) * FACTOR
    d_keys = dot(ds_b, q_wide) * FACTOR
    d_vals = dot(probs_b, d_att_wide)
    att[rows, lane : lane + 128] = attended.astype(BF16)
    d_qkv[rows, lane : lane + 128] = d_query.astype(BF16)
    d_qkv[rows, 512 + lane : 512 + lane + 128] = d_keys.astype(BF16)
    d_qkv[rows, 1024 + lane : 1024 + lane + 128] = d_vals.astype(BF16)


def interleave(units, skew):
    running = []
    time = 0
    units = list(units)
    while units or running:
        if units and time % skew == 0:
            running.append(units.pop(0))
        running = [u for u in running if next(u, True) is not True]
        time += 1


def window_kernel(
    core_ref, x_ref, gain_ref, shift_ref, wqkv_ref, wout_ref, bias_ref, mask_ref, *refs, last
):
    if last:
        gw_in, ln_in, out_ref, mine_ref, other_ref, ln_ref = refs[:6]
        lat_slab, cot_slab, qkv, d_att, d_qkv, att, gw_ref = refs[6:]
    else:
        out_ref, gw_ref, ln_ref = refs[:3]
        lat_slab, cot_slab, qkv, d_att, d_qkv, att = refs[3:]
    windows = x_ref.shape[1] // 2
    step = pl.program_id(0)

    @pl.when(step == 0)
    def _():
        def fill(n, carry):
            rows = pl.ds(pl.multiple_of(n * windows, windows), windows)
            for k in range(4):
                lanes = slice(k * 128, k * 128 + 128)
                lat_slab[k, rows, :] = x_ref[n, :windows, lanes].astype(F32)
                cot_slab[k, rows, :] = x_ref[n, windows:, lanes].astype(F32)
            return carry

        lax.fori_loop(0, CELLS, fill, 0)
        if last:
            gw_ref[...] = gw_in[...]
            ln_ref[...] = ln_in[...]
        else:
            gw_ref[...] = jnp.zeros_like(gw_ref)
            ln_ref[...] = jnp.zeros_like(ln_ref)

    cot = window_rows(cot_slab, step * STEP, windows)
    cot_b = cot.astype(BF16)
    d_att[...] = dot_cols(cot_b, wout_ref[...]).astype(BF16)
    xhat, inverse = standardise(window_rows(lat_slab, step * STEP, windows))
    normed = (xhat * gain_ref[...] + shift_ref[...]).astype(BF16)
    qkv[...] = dot(normed, wqkv_ref[...]).astype(BF16)
    interleave(
        (
            unit(j, g, qkv, d_att, d_qkv, att, bias_ref, mask_ref)
            for j in range(STEP)
            for g in range(GROUPS)
        ),
        SKEW,
    )
    for k in range(3):
        gw_ref[k] += dot_rows(normed, d_qkv[:, k * 512 : k * 512 + 512])
    gw_ref[3] += dot_rows(att[...], cot_b)
    d_normed = dot_cols(d_qkv[...], wqkv_ref[...])
    weighted = xhat * d_normed
    ln_ref[0] += jnp.sum(weighted.reshape(ROWS // 8, 8, 512), 0)
    ln_ref[1] += jnp.sum(d_normed.reshape(ROWS // 8, 8, 512), 0)
    d_hat = d_normed * gain_ref[...]
    value = cot + inverse * (
        d_hat
        - jnp.mean(d_hat, -1, keepdims=True)
        - xhat * jnp.mean(d_hat * xhat, -1, keepdims=True)
    )
    for j in range(STEP):
        for k in range(4):
            lat_slab[k, pl.ds(step * STEP + j, CELLS, stride=windows), :] = value[
                j * CELLS : j * CELLS + CELLS, k * 128 : k * 128 + 128
            ]

    @pl.when(step == pl.num_programs(0) - 1)
    def _():
        def empty(n, carry):
            rows = pl.ds(pl.multiple_of(n * windows, windows), windows)
            for k in range(4):
                out_ref[n, :, k * 128 : k * 128 + 128] = lat_slab[k, rows, :].astype(BF16)
            return carry

        lax.fori_loop(0, CELLS, empty, 0)
        if last:
            core = core_ref[0]
            for k in range(2):
                mine_ref[k] = gw_ref[2 * core + k]
                other_ref[k] = gw_ref[2 * (1 - core) + k].astype(BF16)


def whole(shape):
    return pl.BlockSpec(shape, lambda i: (0,) * len(shape))


def window_pass(core, x, gain, shift, w_qkv, w_out, bias, mask, sums):
    last = sums is not None
    windows = x.shape[1] // 2
    cells = windows * CELLS
    shape = jax.ShapeDtypeStruct
    outs = [shape((CELLS, windows, 512), BF16)]
    if last:
        outs += [shape((2, 512, 512), F32), shape((2, 512, 512), BF16)]
    else:
        outs += [shape((4, 512, 512), F32)]
    outs += [shape((2, 8, 512), F32)]
    operands = (x, gain, shift, w_qkv, w_out, bias, mask) + tuple(sums or ())

    def kernel(*refs):
        window_kernel(*refs, last=last)

    return pl.pallas_call(
        kernel,
        grid=(windows // STEP,),
        in_specs=[pl.BlockSpec(memory_space=pltpu.SMEM)] + [whole(o.shape) for o in operands],
        out_specs=[whole(o.shape) for o in outs],
        out_shape=outs,
        scratch_shapes=[
            pltpu.VMEM((4, cells, 128), F32),
            pltpu.VMEM((4, cells, 128), F32),
            pltpu.VMEM((ROWS, 1536), BF16),
            pltpu.VMEM((ROWS, 512), BF16),
            pltpu.VMEM((ROWS, 1536), BF16),
            pltpu.VMEM((ROWS, 512), BF16),
        ]
        + ([pltpu.VMEM((4, 512, 512), F32)] if last else []),
        compiler_params=pltpu.CompilerParams(vmem_limit_bytes=52 * MIB),
        cost_estimate=pl.CostEstimate(
            flops=25 * 10**9, bytes_accessed=20 * MIB, transcendentals=10**6
        ),
        name="window_last" if last else "window_first",
    )(core, *operands)


def bias_tables(rel_bias):
    position = jnp.arange(CELLS, dtype=jnp.int32)
    prow = position // 8
    pcol = position % 8
    offset = (prow[None, :] - prow[:, None] + 7) * 15 + (pcol[None, :] - pcol[:, None] + 7)
    onehot = (offset.reshape(1, -1) == jnp.arange(225, dtype=jnp.int32)[:, None]).astype(F32)
    full = jnp.dot(rel_bias, onehot, precision=lax.Precision.HIGHEST)
    full = full.reshape(GROUPS, HEADS // GROUPS, CELLS, CELLS).transpose(0, 2, 1, 3)
    return full.reshape(GROUPS, CELLS, 256)


def after(value, *others):
    return lax.optimization_barrier((value,) + others)[0]


def exchange(array):
    return lax.all_to_all(array, ("gx", "gh"), split_axis=0, concat_axis=0, tiled=True)


def swap_cores(array):
    return lax.ppermute(array, "core", [(0, 1), (1, 0)])


def body(latent, cotangent, gain, shift, w_qkv, w_out, rel_bias):
    rows, cols, width = latent.shape
    peers = lax.axis_size("gx") * lax.axis_size("gh")
    windows = rows * cols // peers
    half = windows // PARTS
    norm = 1.0 / math.sqrt(rows * cols * peers * lax.axis_size("core"))
    core = lax.axis_index("core")
    gain = gain.reshape(1, width)
    shift = shift.reshape(1, width)
    lane = jnp.arange(128, dtype=jnp.int32) // 32
    mask = jnp.broadcast_to(
        (lane[None, None, :] == jnp.arange(4, dtype=jnp.int32)[:, None, None]).astype(BF16),
        (4, CELLS, 128),
    )
    bias = bias_tables(rel_bias)
    consts = (gain, shift, w_qkv, w_out, bias, mask)
    core_id = core.astype(jnp.int32).reshape(1)

    latent = latent.reshape(peers, windows, width)
    cotangent = cotangent.reshape(peers, windows, width)
    first = jnp.concatenate([latent[:, :half], cotangent[:, :half]], axis=1)
    second = jnp.concatenate([latent[:, half:], cotangent[:, half:]], axis=1)
    x_first = exchange(first)
    x_second = exchange(after(second, x_first))
    d_first, gw, ln = window_pass(core_id, x_first, *consts, None)
    back_first = exchange(d_first)
    d_second, mine, other, ln = window_pass(core_id, x_second, *consts, (gw, ln))

    ln = jnp.sum(ln, axis=1).reshape(8, 128)
    received = swap_cores(other).astype(F32)
    ln = ln + swap_cores(ln)
    mine = (mine + received).astype(BF16).reshape(peers, 16, width)
    ln = jnp.broadcast_to(jnp.pad(ln, ((0, 8), (0, 0))).astype(BF16)[None], (peers, 16, 128))
    payload = after(jnp.concatenate([d_second, mine, ln], axis=2), back_first)
    moved = exchange(payload)
    total = jnp.sum(moved[:, :, width:].astype(F32), axis=0) * norm
    weights = total[:, :width].astype(BF16)
    full = exchange(jnp.broadcast_to(weights[None], (peers, 16, width)))
    result = jnp.concatenate([back_first, moved[:, :, :width]], axis=1)
    ours = full.reshape(2, width, width)
    theirs = swap_cores(ours)
    low = jnp.where(core == 0, ours, theirs).astype(F32)
    high = jnp.where(core == 0, theirs, ours).astype(F32)
    ln_total = total[:8, width:].reshape(2, width)
    return (
        result.reshape(rows, cols, width),
        jnp.concatenate([low[0], low[1], high[0]], axis=1),
        high[1],
        ln_total[0],
        ln_total[1],
    )


def solution(mesh):
    cores = mesh.devices.reshape(mesh.shape["gx"], mesh.shape["gy"] // 2, 2)
    inner = Mesh(cores, ("gx", "gh", "core"))
    block = P("gx", ("gh", "core"), None)
    return jax.shard_map(
        body,
        mesh=inner,
        in_specs=(block, block, P(), P(), P(), P(), P()),
        out_specs=(block, P(), P(), P(), P()),
        check_vma=False,
    )
```

```python
import math

import jax
import jax.numpy as jnp
from jax import lax
from jax.experimental import pallas as pl
from jax.experimental.pallas import tpu as pltpu
from jax.sharding import Mesh, PartitionSpec as P

F32 = jnp.float32
BF16 = jnp.bfloat16
HEADS = 16
CELLS = 64
PARTS = 2
STEP = 8
ROWS = STEP * CELLS
GROUPS = 4
FACTOR = 1.0 / math.sqrt(32.0)
NATURAL = (0, 1, 2, 3)
SWAPPED = (0, 2, 1, 3)
SKEW = 1
CHUNKS = 4
CHUNK = CELLS // CHUNKS
VMEM_MIB = 60
MIB = 1 << 20


def dot(left, right):
    return jnp.dot(left, right, preferred_element_type=F32)


def dot_cols(left, right):
    return lax.dot_general(left, right, (((1,), (1,)), ((), ())), preferred_element_type=F32)


def dot_rows(left, right):
    return lax.dot_general(left, right, (((0,), (0,)), ((), ())), preferred_element_type=F32)


def spread(block, mask_ref, order):
    return jnp.concatenate([block * mask_ref[h] for h in order], axis=0)


def turn(block):
    tall = jnp.concatenate([block[:, :128], block[:, 128:]], axis=0)
    tall = tall.T
    return jnp.concatenate([tall[:64], tall[64:]], axis=1)


def window_rows(slab, first, windows):
    return jnp.concatenate(
        [
            jnp.concatenate(
                [slab[k, pl.ds(first + j, CELLS, stride=windows), :] for j in range(STEP)], axis=0
            )
            for k in range(4)
        ],
        axis=1,
    )


def standardise(values):
    centred = values - jnp.mean(values, -1, keepdims=True)
    variance = jnp.mean(centred * centred, -1, keepdims=True)
    inverse = lax.rsqrt(variance + 1e-05)
    return centred * inverse, inverse


def unit(j, g, qkv, d_att, d_qkv, att, bias_ref, mask_ref):
    rows = pl.ds(j * CELLS, CELLS)
    lane = g * 128
    q4 = qkv[rows, lane : lane + 128]
    k4 = qkv[rows, 512 + lane : 512 + lane + 128]
    v4 = qkv[rows, 1024 + lane : 1024 + lane + 128]
    q_wide = spread(q4, mask_ref, NATURAL)
    d_att_wide = spread(d_att[rows, lane : lane + 128], mask_ref, NATURAL)
    scores = dot_cols(k4, q_wide) * FACTOR + bias_ref[g]
    d_probs = dot_cols(v4, d_att_wide)
    yield
    probs = jnp.exp(scores - jnp.max(scores, 0, keepdims=True))
    probs = probs * (1.0 / jnp.sum(probs, 0, keepdims=True))
    probs_b = probs.astype(BF16)
    yield
    d_scores = probs * (d_probs - jnp.sum(probs * d_probs, 0, keepdims=True))
    ds_b = d_scores.astype(BF16)
    yield
    turned = turn(probs_b)
    ds_turned = turn(ds_b)
    yield
    attended = dot(turned, spread(v4, mask_ref, SWAPPED))
    d_query = dot(ds_turned, spread(k4, mask_ref, SWAPPED)) * FACTOR
    d_keys = dot(ds_b, q_wide) * FACTOR
    d_vals = dot(probs_b, d_att_wide)
    att[rows, lane : lane + 128] = attended.astype(BF16)
    d_qkv[rows, lane : lane + 128] = d_query.astype(BF16)
    d_qkv[rows, 512 + lane : 512 + lane + 128] = d_keys.astype(BF16)
    d_qkv[rows, 1024 + lane : 1024 + lane + 128] = d_vals.astype(BF16)


def interleave(units, skew):
    running = []
    time = 0
    units = list(units)
    while units or running:
        if units and time % skew == 0:
            running.append(units.pop(0))
        alive = [u for u in reversed(running) if next(u, True) is not True]
        running = alive[::-1]
        time += 1


def copies_in(pairs, sems):
    copies = [
        pltpu.make_async_copy(source, target, sems.at[i])
        for i, (source, target) in enumerate(pairs)
    ]
    for copy in copies:
        copy.start()
    return copies


def chunk_copy(source, target, sems, c):
    part = pl.ds(c * CHUNK, CHUNK)
    return pltpu.make_async_copy(source.at[part], target.at[part], sems.at[c])


def window_kernel(*refs, last):
    core_ref, x_any, gain_ref, shift_ref, wqkv_any, wout_any, bias_any, mask_ref = refs[:8]
    refs = refs[8:]
    if last:
        gw_any, ln_in, out_any, other_any, ln_out = refs[:5]
        other, gw_before, ln_ref = refs[-3:]
        refs = refs[5:-3]
    else:
        out_any, gw_any, ln_ref = refs[:3]
        refs = refs[3:]
    x_ref, wqkv_ref, wout_ref, bias_ref, gw_ref, out_ref = refs[:6]
    lat_slab, cot_slab, qkv, d_att, d_qkv, att, x_sems, sems, out_sems = refs[6:]
    windows = x_ref.shape[1] // 2

    for c in range(CHUNKS):
        chunk_copy(x_any, x_ref, x_sems, c).start()
    pairs = [(wout_any, wout_ref), (wqkv_any, wqkv_ref), (bias_any, bias_ref)]
    if last:
        ln_ref[...] = ln_in[...]
    else:
        ln_ref[...] = jnp.zeros_like(ln_ref)
    loads = copies_in(pairs, sems)
    gw_ref[...] = jnp.zeros_like(gw_ref)

    def fill(c, carry):
        chunk_copy(x_any, x_ref, x_sems, c).wait()
        for i in range(CHUNK):
            n = c * CHUNK + i
            rows = pl.ds(pl.multiple_of(n * windows, windows), windows)
            for k in range(4):
                lanes = slice(k * 128, k * 128 + 128)
                lat_slab[k, rows, :] = x_ref[n, :windows, lanes].astype(F32)
                cot_slab[k, rows, :] = x_ref[n, windows:, lanes].astype(F32)
        return carry

    lax.fori_loop(0, CHUNKS, fill, 0)
    for load in loads:
        load.wait()
    if last:
        before = pltpu.make_async_copy(gw_any, gw_before, sems.at[3])
        before.start()

    def step(t, carry):
        cot = window_rows(cot_slab, t * STEP, windows)
        cot_b = cot.astype(BF16)
        d_att[...] = dot_cols(cot_b, wout_ref[...]).astype(BF16)
        xhat, inverse = standardise(window_rows(lat_slab, t * STEP, windows))
        normed = (xhat * gain_ref[...] + shift_ref[...]).astype(BF16)
        qkv[...] = dot(normed, wqkv_ref[...]).astype(BF16)
        interleave(
            (
                unit(j, g, qkv, d_att, d_qkv, att, bias_ref, mask_ref)
                for j in range(STEP)
                for g in range(GROUPS)
            ),
            SKEW,
        )
        for k in range(3):
            gw_ref[k] += dot_rows(normed, d_qkv[:, k * 512 : k * 512 + 512])
        gw_ref[3] += dot_rows(att[...], cot_b)
        d_normed = dot_cols(d_qkv[...], wqkv_ref[...])
        weighted = xhat * d_normed
        ln_ref[0] += jnp.sum(weighted.reshape(ROWS // 8, 8, 512), 0)
        ln_ref[1] += jnp.sum(d_normed.reshape(ROWS // 8, 8, 512), 0)
        d_hat = d_normed * gain_ref[...]
        value = cot + inverse * (
            d_hat
            - jnp.mean(d_hat, -1, keepdims=True)
            - xhat * jnp.mean(d_hat * xhat, -1, keepdims=True)
        )
        for j in range(STEP):
            for k in range(4):
                lat_slab[k, pl.ds(t * STEP + j, CELLS, stride=windows), :] = value[
                    j * CELLS : j * CELLS + CELLS, k * 128 : k * 128 + 128
                ]
        return carry

    lax.fori_loop(0, windows // STEP, step, 0)

    stores = []
    if last:
        for part in range(2):
            sums = jnp.sum(ln_ref[part], 0, keepdims=True)
            for k in range(4):
                row = part * 4 + k
                ln_out[row : row + 1, :] = sums[:, k * 128 : k * 128 + 128]
        before.wait()
        core = core_ref[0]
        for k in range(2):
            block = 2 * (1 - core) + k
            other[:, k * 512 : k * 512 + 512] = (gw_ref[block] + gw_before[block]).astype(BF16)
        stores.append(pltpu.make_async_copy(other, other_any, sems.at[0]))
    else:
        stores.append(pltpu.make_async_copy(gw_ref, gw_any, sems.at[0]))
    stores[0].start()

    def empty(c, carry):
        for i in range(CHUNK):
            n = c * CHUNK + i
            rows = pl.ds(pl.multiple_of(n * windows, windows), windows)
            for k in range(4):
                cells = lat_slab[k, rows, :].astype(BF16)
                lane = k * 128
                if last:
                    out_ref[n, :, lane : lane + 128] = cells[:8]
                    out_ref[n, :, 512 + lane : 512 + lane + 128] = cells[8:]
                else:
                    out_ref[n, :, lane : lane + 128] = cells
            if last:
                mine = pl.ds(pl.multiple_of(n * 8, 8), 8)
                for k in range(2):
                    block = 2 * core + k
                    out_ref[n, :, 1024 + k * 512 : 1536 + k * 512] = (
                        gw_ref[block, mine, :] + gw_before[block, mine, :]
                    ).astype(BF16)
        chunk_copy(out_ref, out_any, out_sems, c).start()
        return carry

    lax.fori_loop(0, CHUNKS, empty, 0)
    for c in range(CHUNKS):
        stores.append(chunk_copy(out_ref, out_any, out_sems, c))
    for store in stores:
        store.wait()


def window_pass(core, x, gain, shift, w_qkv, w_out, bias, mask, sums):
    last = sums is not None
    windows = x.shape[1] // 2
    cells = windows * CELLS
    shape = jax.ShapeDtypeStruct
    everywhere = pl.BlockSpec(memory_space=pl.ANY)
    vmem = pl.BlockSpec(memory_space=pltpu.VMEM)
    grads = shape((4, 512, 512), F32)
    ln = shape((2, 8, 512), F32)
    if last:
        outs = [shape((CELLS, 8, 2048), BF16), shape((512, 1024), BF16), shape((8, 128), F32)]
    else:
        outs = [shape((CELLS, windows, 512), BF16), grads, ln]

    def kernel(*refs):
        window_kernel(*refs, last=last)

    return pl.pallas_call(
        kernel,
        in_specs=[
            pl.BlockSpec(memory_space=pltpu.SMEM),
            everywhere, vmem, vmem, everywhere, everywhere, everywhere, vmem,
        ]
        + ([everywhere, vmem] if last else []),
        out_specs=[everywhere, everywhere, vmem],
        out_shape=outs,
        scratch_shapes=[
            pltpu.VMEM(x.shape, BF16),
            pltpu.VMEM(w_qkv.shape, BF16),
            pltpu.VMEM(w_out.shape, BF16),
            pltpu.VMEM(bias.shape, F32),
            pltpu.VMEM(grads.shape, F32),
            pltpu.VMEM(outs[0].shape, BF16),
            pltpu.VMEM((4, cells, 128), F32),
            pltpu.VMEM((4, cells, 128), F32),
            pltpu.VMEM((ROWS, 1536), BF16),
            pltpu.VMEM((ROWS, 512), BF16),
            pltpu.VMEM((ROWS, 1536), BF16),
            pltpu.VMEM((ROWS, 512), BF16),
            pltpu.SemaphoreType.DMA((CHUNKS,)),
            pltpu.SemaphoreType.DMA((4,)),
            pltpu.SemaphoreType.DMA((CHUNKS,)),
        ]
        + (
            [
                pltpu.VMEM((512, 1024), BF16),
                pltpu.VMEM(grads.shape, F32),
                pltpu.VMEM(ln.shape, F32),
            ]
            if last
            else []
        ),
        compiler_params=pltpu.CompilerParams(vmem_limit_bytes=VMEM_MIB * MIB),
        cost_estimate=pl.CostEstimate(
            flops=20 * 10**9, bytes_accessed=12 * MIB, transcendentals=10**6
        ),
        name="window_last" if last else "window_first",
    )(core, x, gain, shift, w_qkv, w_out, bias, mask, *(sums or ()))


def pack(latent, cotangent, part, half):
    peers, _, width = latent.shape
    pieces = 4
    size = peers // pieces

    def kernel(latent_any, cotangent_any, out_any, held, in_sems, out_sems):
        def load(c, k):
            block = pl.ds(c * size, size)
            source = (latent_any, cotangent_any)[k]
            return pltpu.make_async_copy(
                source.at[block, pl.ds(part * half, half)],
                held.at[block, pl.ds(k * half, half)],
                in_sems.at[2 * c + k],
            )

        def store(c):
            block = pl.ds(c * size, size)
            return pltpu.make_async_copy(held.at[block], out_any.at[block], out_sems.at[c])

        for c in range(pieces):
            load(c, 0).start()
            load(c, 1).start()
        for c in range(pieces):
            load(c, 0).wait()
            load(c, 1).wait()
            store(c).start()
        for c in range(pieces):
            store(c).wait()

    everywhere = pl.BlockSpec(memory_space=pl.ANY)
    return pl.pallas_call(
        kernel,
        in_specs=[everywhere, everywhere],
        out_specs=everywhere,
        out_shape=jax.ShapeDtypeStruct((peers, 2 * half, width), BF16),
        scratch_shapes=[
            pltpu.VMEM((peers, 2 * half, width), BF16),
            pltpu.SemaphoreType.DMA((2 * pieces,)),
            pltpu.SemaphoreType.DMA((pieces,)),
        ],
        compiler_params=pltpu.CompilerParams(vmem_limit_bytes=VMEM_MIB * MIB),
        cost_estimate=pl.CostEstimate(flops=0, bytes_accessed=4 * MIB, transcendentals=0),
        name="pack_part",
    )(latent, cotangent)


def join_kernel(core_ref, ours_ref, theirs_ref, gq_ref, go_ref):
    own = core_ref[0] == 0
    ours = ours_ref[:, :1024].astype(F32)
    theirs = theirs_ref[:, :1024].astype(F32)
    gq_ref[:, :1024] = jnp.where(own, ours, theirs)
    high = jnp.where(own, theirs, ours)
    gq_ref[:, 1024:] = high[:, :512]
    go_ref[...] = high[:, 512:]


def join(core, ours, theirs):
    def block(width):
        return pl.BlockSpec((128, width), lambda i: (i, 0))

    return pl.pallas_call(
        join_kernel,
        grid=(4,),
        in_specs=[pl.BlockSpec(memory_space=pltpu.SMEM), block(1152), block(1152)],
        out_specs=[block(1536), block(512)],
        out_shape=[
            jax.ShapeDtypeStruct((512, 1536), F32),
            jax.ShapeDtypeStruct((512, 512), F32),
        ],
        compiler_params=pltpu.CompilerParams(vmem_limit_bytes=8 * MIB),
        name="join_halves",
    )(core, ours, theirs)


def bias_tables(rel_bias):
    position = jnp.arange(CELLS, dtype=jnp.int32)
    prow = position // 8
    pcol = position % 8
    offset = (prow[None, :] - prow[:, None] + 7) * 15 + (pcol[None, :] - pcol[:, None] + 7)
    onehot = (offset.reshape(1, -1) == jnp.arange(225, dtype=jnp.int32)[:, None]).astype(F32)
    full = jnp.dot(rel_bias, onehot, precision=lax.Precision.HIGHEST)
    full = full.reshape(GROUPS, HEADS // GROUPS, CELLS, CELLS).transpose(0, 2, 1, 3)
    return full.reshape(GROUPS, CELLS, 256)


def after(value, *others):
    return lax.optimization_barrier((value,) + others)[0]


def exchange(array):
    return lax.all_to_all(array, ("gx", "gh"), split_axis=0, concat_axis=0, tiled=True)


def swap_cores(array):
    return lax.ppermute(array, "core", [(0, 1), (1, 0)])


def body(latent, cotangent, gain, shift, w_qkv, w_out, rel_bias):
    rows, cols, width = latent.shape
    peers = lax.axis_size("gx") * lax.axis_size("gh")
    windows = rows * cols // peers
    half = windows // PARTS
    norm = 1.0 / math.sqrt(rows * cols * peers * lax.axis_size("core"))
    core = lax.axis_index("core")
    gain = gain.reshape(1, width)
    shift = shift.reshape(1, width)
    lane = jnp.arange(128, dtype=jnp.int32) // 32
    mask = jnp.broadcast_to(
        (lane[None, None, :] == jnp.arange(4, dtype=jnp.int32)[:, None, None]).astype(BF16),
        (4, CELLS, 128),
    )
    bias = bias_tables(rel_bias)
    consts = (gain, shift, w_qkv, w_out, bias, mask)
    core_id = core.astype(jnp.int32).reshape(1)

    latent = latent.reshape(peers, windows, width)
    cotangent = cotangent.reshape(peers, windows, width)
    x_first = exchange(pack(latent, cotangent, 0, half))
    x_second = exchange(after(pack(latent, cotangent, 1, half), x_first))
    d_first, gw, ln = window_pass(core_id, x_first, *consts, None)
    back_first = exchange(d_first)
    payload, other, ln = window_pass(core_id, x_second, *consts, (gw, ln))

    other, ln = lax.optimization_barrier((other, ln, back_first))[:2]
    received = swap_cores(other).reshape(peers, 8, 1024)
    ln = ln + swap_cores(ln)
    mine = payload[:, :, 1024:].astype(F32) + received.astype(F32)
    moved = exchange(payload.at[:, :, 1024:].set(mine.astype(BF16)))
    total = jnp.sum(moved[:, :, 1024:].astype(F32), axis=0) * norm
    share = jnp.concatenate([total, ln], axis=1).astype(BF16)
    full = exchange(jnp.broadcast_to(share[None], (peers, 8, 1152)))
    result = jnp.concatenate(
        [back_first, moved[:, :, :width], moved[:, :, width : 2 * width]], axis=1
    )
    full, result = lax.optimization_barrier((full, result))
    ours = full.reshape(width, 1152)
    grad_qkv, grad_out = join(core_id, ours, swap_cores(ours))
    ln_total = (jnp.sum(full[:, :, 1024:].astype(F32), axis=0) * norm).reshape(2, width)
    return (result.reshape(rows, cols, width), grad_qkv, grad_out, ln_total[0], ln_total[1])


def solution(mesh):
    cores = mesh.devices.reshape(mesh.shape["gx"], mesh.shape["gy"] // 2, 2)
    inner = Mesh(cores, ("gx", "gh", "core"))
    block = P("gx", ("gh", "core"), None)
    return jax.shard_map(
        body,
        mesh=inner,
        in_specs=(block, block, P(), P(), P(), P(), P()),
        out_specs=(block, P(), P(), P(), P()),
        check_vma=False,
    )
```

```python
import math

import jax
import jax.numpy as jnp
from jax import lax
from jax.experimental import pallas as pl
from jax.experimental.pallas import tpu as pltpu
from jax.sharding import Mesh, PartitionSpec as P

F32 = jnp.float32
BF16 = jnp.bfloat16
HEADS = 16
CELLS = 64
PARTS = 2
STEP = 8
ROWS = STEP * CELLS
GROUPS = 4
FACTOR = 1.0 / math.sqrt(32.0)
NATURAL = (0, 1, 2, 3)
SWAPPED = (0, 2, 1, 3)
SKEW = 1
CHUNKS = 4
CHUNK = CELLS // CHUNKS
VMEM_MIB = 60
KERNEL_MIB = 44
MIB = 1 << 20


def dot(left, right):
    return jnp.dot(left, right, preferred_element_type=F32)


def dot_cols(left, right):
    return lax.dot_general(left, right, (((1,), (1,)), ((), ())), preferred_element_type=F32)


def dot_rows(left, right):
    return lax.dot_general(left, right, (((0,), (0,)), ((), ())), preferred_element_type=F32)


def spread(block, mask_ref, order):
    return jnp.concatenate([block * mask_ref[h] for h in order], axis=0)


def turn(block):
    tall = jnp.concatenate([block[:, :128], block[:, 128:]], axis=0)
    tall = tall.T
    return jnp.concatenate([tall[:64], tall[64:]], axis=1)


def window_rows(slab, first, windows):
    return jnp.concatenate(
        [
            jnp.concatenate(
                [slab[k, pl.ds(first + j, CELLS, stride=windows), :] for j in range(STEP)], axis=0
            )
            for k in range(4)
        ],
        axis=1,
    )


def standardise(values):
    centred = values - jnp.mean(values, -1, keepdims=True)
    variance = jnp.mean(centred * centred, -1, keepdims=True)
    inverse = lax.rsqrt(variance + 1e-05)
    return centred * inverse, inverse


def unit(j, g, qkv, d_att, d_qkv, att, bias_ref, mask_ref):
    rows = pl.ds(j * CELLS, CELLS)
    lane = g * 128
    q4 = qkv[rows, lane : lane + 128]
    k4 = qkv[rows, 512 + lane : 512 + lane + 128]
    v4 = qkv[rows, 1024 + lane : 1024 + lane + 128]
    q_wide = spread(q4, mask_ref, NATURAL)
    d_att_wide = spread(d_att[rows, lane : lane + 128], mask_ref, NATURAL)
    scores = dot_cols(k4, q_wide) * FACTOR + bias_ref[g]
    d_probs = dot_cols(v4, d_att_wide)
    yield
    probs = jnp.exp(scores - jnp.max(scores, 0, keepdims=True))
    probs = probs * (1.0 / jnp.sum(probs, 0, keepdims=True))
    probs_b = probs.astype(BF16)
    yield
    d_scores = probs * (d_probs - jnp.sum(probs * d_probs, 0, keepdims=True))
    ds_b = d_scores.astype(BF16)
    yield
    turned = turn(probs_b)
    ds_turned = turn(ds_b)
    yield
    attended = dot(turned, spread(v4, mask_ref, SWAPPED))
    d_query = dot(ds_turned, spread(k4, mask_ref, SWAPPED)) * FACTOR
    d_keys = dot(ds_b, q_wide) * FACTOR
    d_vals = dot(probs_b, d_att_wide)
    att[rows, lane : lane + 128] = attended.astype(BF16)
    d_qkv[rows, lane : lane + 128] = d_query.astype(BF16)
    d_qkv[rows, 512 + lane : 512 + lane + 128] = d_keys.astype(BF16)
    d_qkv[rows, 1024 + lane : 1024 + lane + 128] = d_vals.astype(BF16)


def interleave(units, skew):
    running = []
    time = 0
    units = list(units)
    while units or running:
        if units and time % skew == 0:
            running.append(units.pop(0))
        alive = [u for u in reversed(running) if next(u, True) is not True]
        running = alive[::-1]
        time += 1


def chunk_copy(source, target, sems, c):
    part = pl.ds(c * CHUNK, CHUNK)
    return pltpu.make_async_copy(source.at[part], target.at[part], sems.at[c])


def window_kernel(*refs, last):
    core_ref, x_any, gain_ref, shift_ref, wqkv_ref, wout_ref, bias_ref, mask_ref = refs[:8]
    refs = refs[8:]
    if last:
        gw_any, ln_in, out_any, other_any, ln_out = refs[:5]
        other, gw_before, ln_ref = refs[-3:]
        refs = refs[5:-3]
    else:
        out_any, gw_any, ln_ref = refs[:3]
        refs = refs[3:]
    x_ref, gw_ref, out_ref = refs[:3]
    lat_slab, cot_slab, qkv, d_att, d_qkv, att, x_sems, sems, out_sems = refs[3:]
    windows = x_ref.shape[1] // 2

    for c in range(CHUNKS):
        chunk_copy(x_any, x_ref, x_sems, c).start()
    if last:
        ln_ref[...] = ln_in[...]
    else:
        ln_ref[...] = jnp.zeros_like(ln_ref)
    gw_ref[...] = jnp.zeros_like(gw_ref)

    def fill(c, carry):
        chunk_copy(x_any, x_ref, x_sems, c).wait()
        for i in range(CHUNK):
            n = c * CHUNK + i
            rows = pl.ds(pl.multiple_of(n * windows, windows), windows)
            for k in range(4):
                lanes = slice(k * 128, k * 128 + 128)
                lat_slab[k, rows, :] = x_ref[n, :windows, lanes].astype(F32)
                cot_slab[k, rows, :] = x_ref[n, windows:, lanes].astype(F32)
        return carry

    lax.fori_loop(0, CHUNKS, fill, 0)
    if last:
        before = pltpu.make_async_copy(gw_any, gw_before, sems.at[3])
        before.start()

    def step(t, carry):
        cot = window_rows(cot_slab, t * STEP, windows)
        cot_b = cot.astype(BF16)
        d_att[...] = dot_cols(cot_b, wout_ref[...]).astype(BF16)
        xhat, inverse = standardise(window_rows(lat_slab, t * STEP, windows))
        normed = (xhat * gain_ref[...] + shift_ref[...]).astype(BF16)
        qkv[...] = dot(normed, wqkv_ref[...]).astype(BF16)
        interleave(
            (
                unit(j, g, qkv, d_att, d_qkv, att, bias_ref, mask_ref)
                for j in range(STEP)
                for g in range(GROUPS)
            ),
            SKEW,
        )
        for k in range(3):
            gw_ref[k] += dot_rows(normed, d_qkv[:, k * 512 : k * 512 + 512])
        gw_ref[3] += dot_rows(att[...], cot_b)
        d_normed = dot_cols(d_qkv[...], wqkv_ref[...])
        weighted = xhat * d_normed
        ln_ref[0] += jnp.sum(weighted.reshape(ROWS // 8, 8, 512), 0)
        ln_ref[1] += jnp.sum(d_normed.reshape(ROWS // 8, 8, 512), 0)
        d_hat = d_normed * gain_ref[...]
        value = cot + inverse * (
            d_hat
            - jnp.mean(d_hat, -1, keepdims=True)
            - xhat * jnp.mean(d_hat * xhat, -1, keepdims=True)
        )
        for j in range(STEP):
            for k in range(4):
                lat_slab[k, pl.ds(t * STEP + j, CELLS, stride=windows), :] = value[
                    j * CELLS : j * CELLS + CELLS, k * 128 : k * 128 + 128
                ]
        return carry

    lax.fori_loop(0, windows // STEP, step, 0)

    stores = []
    if last:
        for part in range(2):
            sums = jnp.sum(ln_ref[part], 0, keepdims=True)
            for k in range(4):
                row = part * 4 + k
                ln_out[row : row + 1, :] = sums[:, k * 128 : k * 128 + 128]
        before.wait()
        core = core_ref[0]
        for k in range(2):
            block = 2 * (1 - core) + k
            other[:, k * 512 : k * 512 + 512] = (gw_ref[block] + gw_before[block]).astype(BF16)
        stores.append(pltpu.make_async_copy(other, other_any, sems.at[0]))
    else:
        stores.append(pltpu.make_async_copy(gw_ref, gw_any, sems.at[0]))
    stores[0].start()

    def empty(c, carry):
        for i in range(CHUNK):
            n = c * CHUNK + i
            rows = pl.ds(pl.multiple_of(n * windows, windows), windows)
            for k in range(4):
                cells = lat_slab[k, rows, :].astype(BF16)
                lane = k * 128
                if last:
                    out_ref[n, :, lane : lane + 128] = cells[:8]
                    out_ref[n, :, 512 + lane : 512 + lane + 128] = cells[8:]
                else:
                    out_ref[n, :, lane : lane + 128] = cells
            if last:
                mine = pl.ds(pl.multiple_of(n * 8, 8), 8)
                for k in range(2):
                    block = 2 * core + k
                    out_ref[n, :, 1024 + k * 512 : 1536 + k * 512] = (
                        gw_ref[block, mine, :] + gw_before[block, mine, :]
                    ).astype(BF16)
        chunk_copy(out_ref, out_any, out_sems, c).start()
        return carry

    lax.fori_loop(0, CHUNKS, empty, 0)
    for c in range(CHUNKS):
        stores.append(chunk_copy(out_ref, out_any, out_sems, c))
    for store in stores:
        store.wait()


def window_pass(core, x, gain, shift, w_qkv, w_out, bias, mask, sums):
    last = sums is not None
    windows = x.shape[1] // 2
    cells = windows * CELLS
    shape = jax.ShapeDtypeStruct
    hbm = pl.BlockSpec(memory_space=pltpu.HBM)
    vmem = pl.BlockSpec(memory_space=pltpu.VMEM)
    grads = shape((4, 512, 512), F32)
    ln = shape((2, 8, 512), F32)
    if last:
        outs = [shape((CELLS, 8, 2048), BF16), shape((512, 1024), BF16), shape((8, 128), F32)]
    else:
        outs = [shape((CELLS, windows, 512), BF16), grads, ln]

    def kernel(*refs):
        window_kernel(*refs, last=last)

    return pl.pallas_call(
        kernel,
        in_specs=[
            pl.BlockSpec(memory_space=pltpu.SMEM),
            hbm, vmem, vmem, vmem, vmem, vmem, vmem,
        ]
        + ([hbm, vmem] if last else []),
        out_specs=[hbm, hbm, vmem],
        out_shape=outs,
        scratch_shapes=[
            pltpu.VMEM(x.shape, BF16),
            pltpu.VMEM(grads.shape, F32),
            pltpu.VMEM(outs[0].shape, BF16),
            pltpu.VMEM((4, cells, 128), F32),
            pltpu.VMEM((4, cells, 128), F32),
            pltpu.VMEM((ROWS, 1536), BF16),
            pltpu.VMEM((ROWS, 512), BF16),
            pltpu.VMEM((ROWS, 1536), BF16),
            pltpu.VMEM((ROWS, 512), BF16),
            pltpu.SemaphoreType.DMA((CHUNKS,)),
            pltpu.SemaphoreType.DMA((4,)),
            pltpu.SemaphoreType.DMA((CHUNKS,)),
        ]
        + (
            [
                pltpu.VMEM((512, 1024), BF16),
                pltpu.VMEM(grads.shape, F32),
                pltpu.VMEM(ln.shape, F32),
            ]
            if last
            else []
        ),
        compiler_params=pltpu.CompilerParams(vmem_limit_bytes=KERNEL_MIB * MIB),
        cost_estimate=pl.CostEstimate(
            flops=20 * 10**9, bytes_accessed=12 * MIB, transcendentals=10**6
        ),
        name="window_last" if last else "window_first",
    )(core, x, gain, shift, w_qkv, w_out, bias, mask, *(sums or ()))


def stage(*arrays):
    def kernel(*refs):
        count = len(arrays)
        sems = refs[-1]
        copies = [
            pltpu.make_async_copy(refs[i], refs[count + i], sems.at[i]) for i in range(count)
        ]
        for copy in copies:
            copy.start()
        for copy in copies:
            copy.wait()

    return pl.pallas_call(
        kernel,
        in_specs=[pl.BlockSpec(memory_space=pltpu.HBM)] * len(arrays),
        out_specs=[pl.BlockSpec(memory_space=pltpu.VMEM)] * len(arrays),
        out_shape=[jax.ShapeDtypeStruct(a.shape, a.dtype) for a in arrays],
        scratch_shapes=[pltpu.SemaphoreType.DMA((len(arrays),))],
        compiler_params=pltpu.CompilerParams(vmem_limit_bytes=KERNEL_MIB * MIB),
        cost_estimate=pl.CostEstimate(flops=0, bytes_accessed=3 * MIB, transcendentals=0),
        name="stage_constants",
    )(*arrays)


def pack(latent, cotangent, part, half):
    peers, _, width = latent.shape
    pieces = 4
    size = peers // pieces

    def kernel(latent_any, cotangent_any, out_any, held, in_sems, out_sems):
        def load(c, k):
            block = pl.ds(c * size, size)
            source = (latent_any, cotangent_any)[k]
            return pltpu.make_async_copy(
                source.at[block, pl.ds(part * half, half)],
                held.at[block, pl.ds(k * half, half)],
                in_sems.at[2 * c + k],
            )

        def store(c):
            block = pl.ds(c * size, size)
            return pltpu.make_async_copy(held.at[block], out_any.at[block], out_sems.at[c])

        for c in range(pieces):
            load(c, 0).start()
            load(c, 1).start()
        for c in range(pieces):
            load(c, 0).wait()
            load(c, 1).wait()
            store(c).start()
        for c in range(pieces):
            store(c).wait()

    hbm = pl.BlockSpec(memory_space=pltpu.HBM)
    return pl.pallas_call(
        kernel,
        in_specs=[hbm, hbm],
        out_specs=hbm,
        out_shape=jax.ShapeDtypeStruct((peers, 2 * half, width), BF16),
        scratch_shapes=[
            pltpu.VMEM((peers, 2 * half, width), BF16),
            pltpu.SemaphoreType.DMA((2 * pieces,)),
            pltpu.SemaphoreType.DMA((pieces,)),
        ],
        compiler_params=pltpu.CompilerParams(vmem_limit_bytes=VMEM_MIB * MIB),
        cost_estimate=pl.CostEstimate(flops=0, bytes_accessed=4 * MIB, transcendentals=0),
        name="pack_part",
    )(latent, cotangent)


def join_kernel(core_ref, ours_ref, theirs_ref, gq_ref, go_ref):
    own = core_ref[0] == 0
    ours = ours_ref[:, :1024].astype(F32)
    theirs = theirs_ref[:, :1024].astype(F32)
    gq_ref[:, :1024] = jnp.where(own, ours, theirs)
    high = jnp.where(own, theirs, ours)
    gq_ref[:, 1024:] = high[:, :512]
    go_ref[...] = high[:, 512:]


def join(core, ours, theirs):
    def block(width):
        return pl.BlockSpec((128, width), lambda i: (i, 0))

    return pl.pallas_call(
        join_kernel,
        grid=(4,),
        in_specs=[pl.BlockSpec(memory_space=pltpu.SMEM), block(1152), block(1152)],
        out_specs=[block(1536), block(512)],
        out_shape=[
            jax.ShapeDtypeStruct((512, 1536), F32),
            jax.ShapeDtypeStruct((512, 512), F32),
        ],
        compiler_params=pltpu.CompilerParams(vmem_limit_bytes=8 * MIB),
        name="join_halves",
    )(core, ours, theirs)


def bias_tables(rel_bias):
    position = jnp.arange(CELLS, dtype=jnp.int32)
    prow = position // 8
    pcol = position % 8
    offset = (prow[None, :] - prow[:, None] + 7) * 15 + (pcol[None, :] - pcol[:, None] + 7)
    onehot = (offset.reshape(1, -1) == jnp.arange(225, dtype=jnp.int32)[:, None]).astype(F32)
    full = jnp.dot(rel_bias, onehot, precision=lax.Precision.HIGHEST)
    full = full.reshape(GROUPS, HEADS // GROUPS, CELLS, CELLS).transpose(0, 2, 1, 3)
    return full.reshape(GROUPS, CELLS, 256)


def after(value, *others):
    return lax.optimization_barrier((value,) + others)[0]


def exchange(array):
    return lax.all_to_all(array, ("gx", "gh"), split_axis=0, concat_axis=0, tiled=True)


def swap_cores(array):
    return lax.ppermute(array, "core", [(0, 1), (1, 0)])


def body(latent, cotangent, gain, shift, w_qkv, w_out, rel_bias):
    rows, cols, width = latent.shape
    peers = lax.axis_size("gx") * lax.axis_size("gh")
    windows = rows * cols // peers
    half = windows // PARTS
    norm = 1.0 / math.sqrt(rows * cols * peers * lax.axis_size("core"))
    core = lax.axis_index("core")
    gain = gain.reshape(1, width)
    shift = shift.reshape(1, width)
    lane = jnp.arange(128, dtype=jnp.int32) // 32
    mask = jnp.broadcast_to(
        (lane[None, None, :] == jnp.arange(4, dtype=jnp.int32)[:, None, None]).astype(BF16),
        (4, CELLS, 128),
    )
    bias = bias_tables(rel_bias)
    w_qkv, w_out, bias, mask = stage(w_qkv, w_out, bias, mask)
    consts = (gain, shift, w_qkv, w_out, bias, mask)
    core_id = core.astype(jnp.int32).reshape(1)

    latent = latent.reshape(peers, windows, width)
    cotangent = cotangent.reshape(peers, windows, width)
    x_first = exchange(pack(latent, cotangent, 0, half))
    x_second = exchange(after(pack(latent, cotangent, 1, half), x_first))
    d_first, gw, ln = window_pass(core_id, x_first, *consts, None)
    back_first = exchange(d_first)
    payload, other, ln = window_pass(core_id, x_second, *consts, (gw, ln))

    other, ln = lax.optimization_barrier((other, ln, back_first))[:2]
    received = swap_cores(other).reshape(peers, 8, 1024)
    ln = ln + swap_cores(ln)
    mine = payload[:, :, 1024:].astype(F32) + received.astype(F32)
    moved = exchange(payload.at[:, :, 1024:].set(mine.astype(BF16)))
    total = jnp.sum(moved[:, :, 1024:].astype(F32), axis=0) * norm
    share = jnp.concatenate([total, ln], axis=1).astype(BF16)
    full = exchange(jnp.broadcast_to(share[None], (peers, 8, 1152)))
    result = jnp.concatenate(
        [back_first, moved[:, :, :width], moved[:, :, width : 2 * width]], axis=1
    )
    full, result = lax.optimization_barrier((full, result))
    ours = full.reshape(width, 1152)
    grad_qkv, grad_out = join(core_id, ours, swap_cores(ours))
    ln_total = (jnp.sum(full[:, :, 1024:].astype(F32), axis=0) * norm).reshape(2, width)
    return (result.reshape(rows, cols, width), grad_qkv, grad_out, ln_total[0], ln_total[1])


def solution(mesh):
    cores = mesh.devices.reshape(mesh.shape["gx"], mesh.shape["gy"] // 2, 2)
    inner = Mesh(cores, ("gx", "gh", "core"))
    block = P("gx", ("gh", "core"), None)
    return jax.shard_map(
        body,
        mesh=inner,
        in_specs=(block, block, P(), P(), P(), P(), P()),
        out_specs=(block, P(), P(), P(), P()),
        check_vma=False,
    )
```

```python
import math

import jax
import jax.numpy as jnp
from jax import lax
from jax.experimental import pallas as pl
from jax.experimental.pallas import tpu as pltpu
from jax.sharding import Mesh, PartitionSpec as P

F32 = jnp.float32
BF16 = jnp.bfloat16
HEADS = 16
CELLS = 64
PARTS = 2
STEP = 8
ROWS = STEP * CELLS
GROUPS = 4
FACTOR = 1.0 / math.sqrt(32.0)
NATURAL = (0, 1, 2, 3)
SWAPPED = (0, 2, 1, 3)
SKEW = 1
CHUNKS = 4
CHUNK = CELLS // CHUNKS
VMEM_MIB = 60
KERNEL_MIB = 44
MIB = 1 << 20


def dot(left, right):
    return jnp.dot(left, right, preferred_element_type=F32)


def dot_cols(left, right):
    return lax.dot_general(left, right, (((1,), (1,)), ((), ())), preferred_element_type=F32)


def dot_rows(left, right):
    return lax.dot_general(left, right, (((0,), (0,)), ((), ())), preferred_element_type=F32)


def spread(block, mask_ref, order):
    return jnp.concatenate([block * mask_ref[h] for h in order], axis=0)


def turn(block):
    tall = jnp.concatenate([block[:, :128], block[:, 128:]], axis=0)
    tall = tall.T
    return jnp.concatenate([tall[:64], tall[64:]], axis=1)


def window_rows(slab, first, windows):
    return jnp.concatenate(
        [
            jnp.concatenate(
                [slab[k, pl.ds(first + j, CELLS, stride=windows), :] for j in range(STEP)], axis=0
            )
            for k in range(4)
        ],
        axis=1,
    )


def standardise(values):
    centred = values - jnp.mean(values, -1, keepdims=True)
    variance = jnp.mean(centred * centred, -1, keepdims=True)
    inverse = lax.rsqrt(variance + 1e-05)
    return centred * inverse, inverse


def unit(j, g, qkv, d_att, d_qkv, att, bias_ref, mask_ref):
    rows = pl.ds(j * CELLS, CELLS)
    lane = g * 128
    q4 = qkv[rows, lane : lane + 128]
    k4 = qkv[rows, 512 + lane : 512 + lane + 128]
    v4 = qkv[rows, 1024 + lane : 1024 + lane + 128]
    q_wide = spread(q4, mask_ref, NATURAL)
    d_att_wide = spread(d_att[rows, lane : lane + 128], mask_ref, NATURAL)
    scores = dot_cols(k4, q_wide) * FACTOR + bias_ref[g]
    d_probs = dot_cols(v4, d_att_wide)
    yield
    probs = jnp.exp(scores - jnp.max(scores, 0, keepdims=True))
    probs = probs * (1.0 / jnp.sum(probs, 0, keepdims=True))
    probs_b = probs.astype(BF16)
    yield
    d_scores = probs * (d_probs - jnp.sum(probs * d_probs, 0, keepdims=True))
    ds_b = d_scores.astype(BF16)
    yield
    turned = turn(probs_b)
    ds_turned = turn(ds_b)
    yield
    attended = dot(turned, spread(v4, mask_ref, SWAPPED))
    d_query = dot(ds_turned, spread(k4, mask_ref, SWAPPED)) * FACTOR
    d_keys = dot(ds_b, q_wide) * FACTOR
    d_vals = dot(probs_b, d_att_wide)
    att[rows, lane : lane + 128] = attended.astype(BF16)
    d_qkv[rows, lane : lane + 128] = d_query.astype(BF16)
    d_qkv[rows, 512 + lane : 512 + lane + 128] = d_keys.astype(BF16)
    d_qkv[rows, 1024 + lane : 1024 + lane + 128] = d_vals.astype(BF16)


def interleave(units, skew):
    running = []
    time = 0
    units = list(units)
    while units or running:
        if units and time % skew == 0:
            running.append(units.pop(0))
        alive = [u for u in reversed(running) if next(u, True) is not True]
        running = alive[::-1]
        time += 1


def chunk_copy(source, target, sems, c):
    part = pl.ds(c * CHUNK, CHUNK)
    return pltpu.make_async_copy(source.at[part], target.at[part], sems.at[c])


def window_kernel(*refs, last):
    core_ref, x_any, gain_ref, shift_ref, wqkv_ref, wout_ref, bias_ref, mask_ref = refs[:8]
    refs = refs[8:]
    if last:
        gw_any, ln_in, out_any, other_any, ln_out = refs[:5]
        other, gw_before, ln_ref = refs[-3:]
        refs = refs[5:-3]
    else:
        out_any, gw_any, ln_ref = refs[:3]
        refs = refs[3:]
    x_ref, gw_ref, out_ref = refs[:3]
    lat_slab, cot_slab, qkv, d_att, d_qkv, att, x_sems, sems, out_sems = refs[3:]
    windows = x_ref.shape[1] // 2

    for c in range(CHUNKS):
        chunk_copy(x_any, x_ref, x_sems, c).start()
    if last:
        ln_ref[...] = ln_in[...]
    else:
        ln_ref[...] = jnp.zeros_like(ln_ref)
    gw_ref[...] = jnp.zeros_like(gw_ref)

    def fill(c, carry):
        chunk_copy(x_any, x_ref, x_sems, c).wait()
        for i in range(CHUNK):
            n = c * CHUNK + i
            rows = pl.ds(pl.multiple_of(n * windows, windows), windows)
            for k in range(4):
                lanes = slice(k * 128, k * 128 + 128)
                lat_slab[k, rows, :] = x_ref[n, :windows, lanes].astype(F32)
                cot_slab[k, rows, :] = x_ref[n, windows:, lanes].astype(F32)
        return carry

    lax.fori_loop(0, CHUNKS, fill, 0)
    if last:
        before = pltpu.make_async_copy(gw_any, gw_before, sems.at[3])
        before.start()

    def step(t, carry):
        cot = window_rows(cot_slab, t * STEP, windows)
        cot_b = cot.astype(BF16)
        d_att[...] = dot_cols(cot_b, wout_ref[...]).astype(BF16)
        xhat, inverse = standardise(window_rows(lat_slab, t * STEP, windows))
        normed = (xhat * gain_ref[...] + shift_ref[...]).astype(BF16)
        qkv[...] = dot(normed, wqkv_ref[...]).astype(BF16)
        interleave(
            (
                unit(j, g, qkv, d_att, d_qkv, att, bias_ref, mask_ref)
                for j in range(STEP)
                for g in range(GROUPS)
            ),
            SKEW,
        )
        for k in range(3):
            gw_ref[k] += dot_rows(normed, d_qkv[:, k * 512 : k * 512 + 512])
        gw_ref[3] += dot_rows(att[...], cot_b)
        d_normed = dot_cols(d_qkv[...], wqkv_ref[...])
        weighted = xhat * d_normed
        ln_ref[0] += jnp.sum(weighted.reshape(ROWS // 8, 8, 512), 0)
        ln_ref[1] += jnp.sum(d_normed.reshape(ROWS // 8, 8, 512), 0)
        d_hat = d_normed * gain_ref[...]
        value = cot + inverse * (
            d_hat
            - jnp.mean(d_hat, -1, keepdims=True)
            - xhat * jnp.mean(d_hat * xhat, -1, keepdims=True)
        )
        for j in range(STEP):
            for k in range(4):
                lat_slab[k, pl.ds(t * STEP + j, CELLS, stride=windows), :] = value[
                    j * CELLS : j * CELLS + CELLS, k * 128 : k * 128 + 128
                ]
        return carry

    lax.fori_loop(0, windows // STEP, step, 0)

    stores = []
    if last:
        for part in range(2):
            sums = jnp.sum(ln_ref[part], 0, keepdims=True)
            for k in range(4):
                row = part * 4 + k
                ln_out[row : row + 1, :] = sums[:, k * 128 : k * 128 + 128]
        before.wait()
        core = core_ref[0]
        for k in range(2):
            block = 2 * (1 - core) + k
            other[:, k * 512 : k * 512 + 512] = (gw_ref[block] + gw_before[block]).astype(BF16)
        stores.append(pltpu.make_async_copy(other, other_any, sems.at[0]))
    else:
        stores.append(pltpu.make_async_copy(gw_ref, gw_any, sems.at[0]))
    stores[0].start()

    def empty(c, carry):
        for i in range(CHUNK):
            n = c * CHUNK + i
            rows = pl.ds(pl.multiple_of(n * windows, windows), windows)
            for k in range(4):
                cells = lat_slab[k, rows, :].astype(BF16)
                lane = k * 128
                if last:
                    out_ref[n, :, lane : lane + 128] = cells[:8]
                    out_ref[n, :, 512 + lane : 512 + lane + 128] = cells[8:]
                else:
                    out_ref[n, :, lane : lane + 128] = cells
            if last:
                mine = pl.ds(pl.multiple_of(n * 8, 8), 8)
                for k in range(2):
                    block = 2 * core + k
                    out_ref[n, :, 1024 + k * 512 : 1536 + k * 512] = (
                        gw_ref[block, mine, :] + gw_before[block, mine, :]
                    ).astype(BF16)
        chunk_copy(out_ref, out_any, out_sems, c).start()
        return carry

    lax.fori_loop(0, CHUNKS, empty, 0)
    for c in range(CHUNKS):
        stores.append(chunk_copy(out_ref, out_any, out_sems, c))
    for store in stores:
        store.wait()


def window_pass(core, x, gain, shift, w_qkv, w_out, bias, mask, sums):
    last = sums is not None
    windows = x.shape[1] // 2
    cells = windows * CELLS
    shape = jax.ShapeDtypeStruct
    hbm = pl.BlockSpec(memory_space=pltpu.HBM)
    vmem = pl.BlockSpec(memory_space=pltpu.VMEM)
    grads = shape((4, 512, 512), F32)
    ln = shape((2, 8, 512), F32)
    if last:
        outs = [shape((CELLS, 8, 2048), BF16), shape((512, 1024), BF16), shape((8, 128), F32)]
    else:
        outs = [shape((CELLS, windows, 512), BF16), grads, ln]

    def kernel(*refs):
        window_kernel(*refs, last=last)

    return pl.pallas_call(
        kernel,
        in_specs=[
            pl.BlockSpec(memory_space=pltpu.SMEM),
            hbm, vmem, vmem, vmem, vmem, vmem, vmem,
        ]
        + ([hbm, vmem] if last else []),
        out_specs=[hbm, hbm, vmem],
        out_shape=outs,
        scratch_shapes=[
            pltpu.VMEM(x.shape, BF16),
            pltpu.VMEM(grads.shape, F32),
            pltpu.VMEM(outs[0].shape, BF16),
            pltpu.VMEM((4, cells, 128), F32),
            pltpu.VMEM((4, cells, 128), F32),
            pltpu.VMEM((ROWS, 1536), BF16),
            pltpu.VMEM((ROWS, 512), BF16),
            pltpu.VMEM((ROWS, 1536), BF16),
            pltpu.VMEM((ROWS, 512), BF16),
            pltpu.SemaphoreType.DMA((CHUNKS,)),
            pltpu.SemaphoreType.DMA((4,)),
            pltpu.SemaphoreType.DMA((CHUNKS,)),
        ]
        + (
            [
                pltpu.VMEM((512, 1024), BF16),
                pltpu.VMEM(grads.shape, F32),
                pltpu.VMEM(ln.shape, F32),
            ]
            if last
            else []
        ),
        compiler_params=pltpu.CompilerParams(vmem_limit_bytes=KERNEL_MIB * MIB),
        cost_estimate=pl.CostEstimate(
            flops=20 * 10**9, bytes_accessed=12 * MIB, transcendentals=10**6
        ),
        name="window_last" if last else "window_first",
    )(core, x, gain, shift, w_qkv, w_out, bias, mask, *(sums or ()))


def stage(*arrays):
    def kernel(*refs):
        count = len(arrays)
        sems = refs[-1]
        copies = [
            pltpu.make_async_copy(refs[i], refs[count + i], sems.at[i]) for i in range(count)
        ]
        for copy in copies:
            copy.start()
        for copy in copies:
            copy.wait()

    return pl.pallas_call(
        kernel,
        in_specs=[pl.BlockSpec(memory_space=pltpu.HBM)] * len(arrays),
        out_specs=[pl.BlockSpec(memory_space=pltpu.VMEM)] * len(arrays),
        out_shape=[jax.ShapeDtypeStruct(a.shape, a.dtype) for a in arrays],
        scratch_shapes=[pltpu.SemaphoreType.DMA((len(arrays),))],
        compiler_params=pltpu.CompilerParams(vmem_limit_bytes=KERNEL_MIB * MIB),
        cost_estimate=pl.CostEstimate(flops=0, bytes_accessed=3 * MIB, transcendentals=0),
        name="stage_constants",
    )(*arrays)


def pack(latent, cotangent, part, half):
    peers, _, width = latent.shape
    pieces = 4
    size = peers // pieces

    def kernel(latent_any, cotangent_any, out_any, held, in_sems, out_sems):
        def load(c, k):
            block = pl.ds(c * size, size)
            source = (latent_any, cotangent_any)[k]
            return pltpu.make_async_copy(
                source.at[block, pl.ds(part * half, half)],
                held.at[block, pl.ds(k * half, half)],
                in_sems.at[2 * c + k],
            )

        def store(c):
            block = pl.ds(c * size, size)
            return pltpu.make_async_copy(held.at[block], out_any.at[block], out_sems.at[c])

        for c in range(pieces):
            load(c, 0).start()
            load(c, 1).start()
        for c in range(pieces):
            load(c, 0).wait()
            load(c, 1).wait()
            store(c).start()
        for c in range(pieces):
            store(c).wait()

    hbm = pl.BlockSpec(memory_space=pltpu.HBM)
    return pl.pallas_call(
        kernel,
        in_specs=[hbm, hbm],
        out_specs=hbm,
        out_shape=jax.ShapeDtypeStruct((peers, 2 * half, width), BF16),
        scratch_shapes=[
            pltpu.VMEM((peers, 2 * half, width), BF16),
            pltpu.SemaphoreType.DMA((2 * pieces,)),
            pltpu.SemaphoreType.DMA((pieces,)),
        ],
        compiler_params=pltpu.CompilerParams(vmem_limit_bytes=VMEM_MIB * MIB),
        cost_estimate=pl.CostEstimate(flops=0, bytes_accessed=4 * MIB, transcendentals=0),
        name="pack_part",
    )(latent, cotangent)


def place_kernel(core_ref, half_ref, *refs, own):
    gq_any, go_any, wide, sems = refs[-4:]
    low = core_ref[0] == (0 if own else 1)
    pieces = 4
    size = wide.shape[0] // pieces

    def copies(p):
        rows = pl.ds(p * size, size)
        first = pltpu.make_async_copy(
            wide.at[rows], gq_any.at[rows, pl.ds(0, 1024)], sems.at[p]
        )
        second = pltpu.make_async_copy(
            wide.at[rows, pl.ds(0, 512)], gq_any.at[rows, pl.ds(1024, 512)], sems.at[p]
        )
        third = pltpu.make_async_copy(
            wide.at[rows, pl.ds(512, 512)], go_any.at[rows], sems.at[pieces + p]
        )
        return first, second, third

    for p in range(pieces):
        rows = pl.ds(p * size, size)
        wide[rows, :] = half_ref[rows, :1024].astype(F32)

        @pl.when(low)
        def _():
            copies(p)[0].start()

        @pl.when(jnp.logical_not(low))
        def _():
            copies(p)[1].start()
            copies(p)[2].start()

    for p in range(pieces):

        @pl.when(low)
        def _():
            copies(p)[0].wait()

        @pl.when(jnp.logical_not(low))
        def _():
            copies(p)[1].wait()
            copies(p)[2].wait()


def place(core, half, placed):
    own = placed is None
    hbm = pl.BlockSpec(memory_space=pltpu.HBM)

    def kernel(*refs):
        place_kernel(*refs, own=own)

    return pl.pallas_call(
        kernel,
        in_specs=[
            pl.BlockSpec(memory_space=pltpu.SMEM),
            pl.BlockSpec(memory_space=pltpu.VMEM),
        ]
        + ([] if own else [hbm, hbm]),
        out_specs=[hbm, hbm],
        out_shape=[
            jax.ShapeDtypeStruct((512, 1536), F32),
            jax.ShapeDtypeStruct((512, 512), F32),
        ],
        scratch_shapes=[pltpu.VMEM((512, 1024), F32), pltpu.SemaphoreType.DMA((8,))],
        input_output_aliases={} if own else {2: 0, 3: 1},
        compiler_params=pltpu.CompilerParams(vmem_limit_bytes=16 * MIB),
        cost_estimate=pl.CostEstimate(flops=0, bytes_accessed=3 * MIB, transcendentals=0),
        name="place_own" if own else "place_other",
    )(core, half, *(placed or ()))


def bias_tables(rel_bias):
    position = jnp.arange(CELLS, dtype=jnp.int32)
    prow = position // 8
    pcol = position % 8
    offset = (prow[None, :] - prow[:, None] + 7) * 15 + (pcol[None, :] - pcol[:, None] + 7)
    onehot = (offset.reshape(1, -1) == jnp.arange(225, dtype=jnp.int32)[:, None]).astype(F32)
    full = jnp.dot(rel_bias, onehot, precision=lax.Precision.HIGHEST)
    full = full.reshape(GROUPS, HEADS // GROUPS, CELLS, CELLS).transpose(0, 2, 1, 3)
    return full.reshape(GROUPS, CELLS, 256)


def after(value, *others):
    return lax.optimization_barrier((value,) + others)[0]


def exchange(array):
    return lax.all_to_all(array, ("gx", "gh"), split_axis=0, concat_axis=0, tiled=True)


def swap_cores(array):
    return lax.ppermute(array, "core", [(0, 1), (1, 0)])


def body(latent, cotangent, gain, shift, w_qkv, w_out, rel_bias):
    rows, cols, width = latent.shape
    peers = lax.axis_size("gx") * lax.axis_size("gh")
    windows = rows * cols // peers
    half = windows // PARTS
    norm = 1.0 / math.sqrt(rows * cols * peers * lax.axis_size("core"))
    core = lax.axis_index("core")
    gain = gain.reshape(1, width)
    shift = shift.reshape(1, width)
    lane = jnp.arange(128, dtype=jnp.int32) // 32
    mask = jnp.broadcast_to(
        (lane[None, None, :] == jnp.arange(4, dtype=jnp.int32)[:, None, None]).astype(BF16),
        (4, CELLS, 128),
    )
    bias = bias_tables(rel_bias)
    w_qkv, w_out, bias, mask = stage(w_qkv, w_out, bias, mask)
    consts = (gain, shift, w_qkv, w_out, bias, mask)
    core_id = core.astype(jnp.int32).reshape(1)

    latent = latent.reshape(peers, windows, width)
    cotangent = cotangent.reshape(peers, windows, width)
    x_first = exchange(pack(latent, cotangent, 0, half))
    x_second = exchange(after(pack(latent, cotangent, 1, half), x_first))
    d_first, gw, ln = window_pass(core_id, x_first, *consts, None)
    back_first = exchange(d_first)
    payload, other, ln = window_pass(core_id, x_second, *consts, (gw, ln))

    other, ln = lax.optimization_barrier((other, ln, back_first))[:2]
    received = swap_cores(other).reshape(peers, 8, 1024)
    ln = ln + swap_cores(ln)
    mine = payload[:, :, 1024:].astype(F32) + received.astype(F32)
    moved = exchange(payload.at[:, :, 1024:].set(mine.astype(BF16)))
    total = jnp.sum(moved[:, :, 1024:].astype(F32), axis=0) * norm
    share = jnp.concatenate([total, ln], axis=1).astype(BF16)
    full = exchange(jnp.broadcast_to(share[None], (peers, 8, 1152)))
    result = jnp.concatenate(
        [back_first, moved[:, :, :width], moved[:, :, width : 2 * width]], axis=1
    )
    full, result = lax.optimization_barrier((full, result))
    ours = full.reshape(width, 1152)
    theirs = swap_cores(ours)
    placed = place(core_id, ours, None)
    grad_qkv, grad_out = place(core_id, theirs, placed)
    ln_total = (jnp.sum(full[:, :, 1024:].astype(F32), axis=0) * norm).reshape(2, width)
    return (result.reshape(rows, cols, width), grad_qkv, grad_out, ln_total[0], ln_total[1])


def solution(mesh):
    cores = mesh.devices.reshape(mesh.shape["gx"], mesh.shape["gy"] // 2, 2)
    inner = Mesh(cores, ("gx", "gh", "core"))
    block = P("gx", ("gh", "core"), None)
    return jax.shard_map(
        body,
        mesh=inner,
        in_specs=(block, block, P(), P(), P(), P(), P()),
        out_specs=(block, P(), P(), P(), P()),
        check_vma=False,
    )
```

```python
import math

import jax
import jax.numpy as jnp
from jax import lax
from jax.experimental import pallas as pl
from jax.experimental.pallas import tpu as pltpu
from jax.sharding import Mesh, PartitionSpec as P

F32 = jnp.float32
BF16 = jnp.bfloat16
HEADS = 16
CELLS = 64
PARTS = 2
STEP = 8
ROWS = STEP * CELLS
GROUPS = 4
FACTOR = 1.0 / math.sqrt(32.0)
NATURAL = (0, 1, 2, 3)
SWAPPED = (0, 2, 1, 3)
SKEW = 1
CHUNKS = 4
CHUNK = CELLS // CHUNKS
VMEM_MIB = 60
KERNEL_MIB = 44
MIB = 1 << 20


def dot(left, right):
    return jnp.dot(left, right, preferred_element_type=F32)


def dot_cols(left, right):
    return lax.dot_general(left, right, (((1,), (1,)), ((), ())), preferred_element_type=F32)


def dot_rows(left, right):
    return lax.dot_general(left, right, (((0,), (0,)), ((), ())), preferred_element_type=F32)


def spread(block, mask_ref, order):
    return jnp.concatenate([block * mask_ref[h] for h in order], axis=0)


def turn(block):
    tall = jnp.concatenate([block[:, :128], block[:, 128:]], axis=0)
    tall = tall.T
    return jnp.concatenate([tall[:64], tall[64:]], axis=1)


def window_rows(slab, first, windows):
    return jnp.concatenate(
        [
            jnp.concatenate(
                [slab[k, pl.ds(first + j, CELLS, stride=windows), :] for j in range(STEP)], axis=0
            )
            for k in range(4)
        ],
        axis=1,
    )


def standardise(values):
    centred = values - jnp.mean(values, -1, keepdims=True)
    variance = jnp.mean(centred * centred, -1, keepdims=True)
    inverse = lax.rsqrt(variance + 1e-05)
    return centred * inverse, inverse


def unit(j, g, qkv, d_att, d_qkv, att, bias_ref, mask_ref):
    rows = pl.ds(j * CELLS, CELLS)
    lane = g * 128
    q4 = qkv[rows, lane : lane + 128]
    k4 = qkv[rows, 512 + lane : 512 + lane + 128]
    v4 = qkv[rows, 1024 + lane : 1024 + lane + 128]
    q_wide = spread(q4, mask_ref, NATURAL)
    d_att_wide = spread(d_att[rows, lane : lane + 128], mask_ref, NATURAL)
    scores = dot_cols(k4, q_wide) * FACTOR + bias_ref[g]
    d_probs = dot_cols(v4, d_att_wide)
    yield
    probs = jnp.exp(scores - jnp.max(scores, 0, keepdims=True))
    probs = probs * (1.0 / jnp.sum(probs, 0, keepdims=True))
    probs_b = probs.astype(BF16)
    yield
    d_scores = probs * (d_probs - jnp.sum(probs * d_probs, 0, keepdims=True))
    ds_b = d_scores.astype(BF16)
    yield
    turned = turn(probs_b)
    ds_turned = turn(ds_b)
    yield
    attended = dot(turned, spread(v4, mask_ref, SWAPPED))
    d_query = dot(ds_turned, spread(k4, mask_ref, SWAPPED)) * FACTOR
    d_keys = dot(ds_b, q_wide) * FACTOR
    d_vals = dot(probs_b, d_att_wide)
    att[rows, lane : lane + 128] = attended.astype(BF16)
    d_qkv[rows, lane : lane + 128] = d_query.astype(BF16)
    d_qkv[rows, 512 + lane : 512 + lane + 128] = d_keys.astype(BF16)
    d_qkv[rows, 1024 + lane : 1024 + lane + 128] = d_vals.astype(BF16)


def interleave(units, skew):
    running = []
    time = 0
    units = list(units)
    while units or running:
        if units and time % skew == 0:
            running.append(units.pop(0))
        alive = [u for u in reversed(running) if next(u, True) is not True]
        running = alive[::-1]
        time += 1


def chunk_copy(source, target, sems, c):
    part = pl.ds(c * CHUNK, CHUNK)
    return pltpu.make_async_copy(source.at[part], target.at[part], sems.at[c])


def window_kernel(*refs, last):
    core_ref, x_any, gain_ref, shift_ref, wqkv_ref, wout_ref, bias_ref, mask_ref = refs[:8]
    refs = refs[8:]
    if last:
        gw_any, ln_in, out_any, other_any, ln_out = refs[:5]
        other, gw_before, ln_ref = refs[-3:]
        refs = refs[5:-3]
    else:
        out_any, gw_any, ln_ref = refs[:3]
        refs = refs[3:]
    x_ref, gw_ref, out_ref = refs[:3]
    lat_slab, cot_slab, qkv, d_att, d_qkv, att, x_sems, sems, out_sems = refs[3:]
    windows = x_ref.shape[1] // 2

    for c in range(CHUNKS):
        chunk_copy(x_any, x_ref, x_sems, c).start()
    if last:
        ln_ref[...] = ln_in[...]
    else:
        ln_ref[...] = jnp.zeros_like(ln_ref)
    gw_ref[...] = jnp.zeros_like(gw_ref)

    def fill(c, carry):
        chunk_copy(x_any, x_ref, x_sems, c).wait()
        for i in range(CHUNK):
            n = c * CHUNK + i
            rows = pl.ds(pl.multiple_of(n * windows, windows), windows)
            for k in range(4):
                lanes = slice(k * 128, k * 128 + 128)
                lat_slab[k, rows, :] = x_ref[n, :windows, lanes].astype(F32)
                cot_slab[k, rows, :] = x_ref[n, windows:, lanes].astype(F32)
        return carry

    lax.fori_loop(0, CHUNKS, fill, 0)
    if last:
        before = pltpu.make_async_copy(gw_any, gw_before, sems.at[3])
        before.start()

    def step(t, carry):
        cot = window_rows(cot_slab, t * STEP, windows)
        cot_b = cot.astype(BF16)
        d_att[...] = dot_cols(cot_b, wout_ref[...]).astype(BF16)
        xhat, inverse = standardise(window_rows(lat_slab, t * STEP, windows))
        normed = (xhat * gain_ref[...] + shift_ref[...]).astype(BF16)
        qkv[...] = dot(normed, wqkv_ref[...]).astype(BF16)
        interleave(
            (
                unit(j, g, qkv, d_att, d_qkv, att, bias_ref, mask_ref)
                for j in range(STEP)
                for g in range(GROUPS)
            ),
            SKEW,
        )
        for k in range(3):
            gw_ref[k] += dot_rows(normed, d_qkv[:, k * 512 : k * 512 + 512])
        gw_ref[3] += dot_rows(att[...], cot_b)
        d_normed = dot_cols(d_qkv[...], wqkv_ref[...])
        weighted = xhat * d_normed
        ln_ref[0] += jnp.sum(weighted.reshape(ROWS // 8, 8, 512), 0)
        ln_ref[1] += jnp.sum(d_normed.reshape(ROWS // 8, 8, 512), 0)
        d_hat = d_normed * gain_ref[...]
        value = cot + inverse * (
            d_hat
            - jnp.mean(d_hat, -1, keepdims=True)
            - xhat * jnp.mean(d_hat * xhat, -1, keepdims=True)
        )
        for j in range(STEP):
            for k in range(4):
                lat_slab[k, pl.ds(t * STEP + j, CELLS, stride=windows), :] = value[
                    j * CELLS : j * CELLS + CELLS, k * 128 : k * 128 + 128
                ]
        return carry

    lax.fori_loop(0, windows // STEP, step, 0)

    stores = []
    if last:
        for part in range(2):
            sums = jnp.sum(ln_ref[part], 0, keepdims=True)
            for k in range(4):
                row = part * 4 + k
                ln_out[row : row + 1, :] = sums[:, k * 128 : k * 128 + 128]
        before.wait()
        core = core_ref[0]
        for k in range(2):
            block = 2 * (1 - core) + k
            other[:, k * 512 : k * 512 + 512] = (gw_ref[block] + gw_before[block]).astype(BF16)
        stores.append(pltpu.make_async_copy(other, other_any, sems.at[0]))
    else:
        stores.append(pltpu.make_async_copy(gw_ref, gw_any, sems.at[0]))
    stores[0].start()

    def empty(c, carry):
        for i in range(CHUNK):
            n = c * CHUNK + i
            rows = pl.ds(pl.multiple_of(n * windows, windows), windows)
            for k in range(4):
                cells = lat_slab[k, rows, :].astype(BF16)
                lane = k * 128
                if last:
                    out_ref[n, :, lane : lane + 128] = cells[:8]
                    out_ref[n, :, 512 + lane : 512 + lane + 128] = cells[8:]
                else:
                    out_ref[n, :, lane : lane + 128] = cells
            if last:
                mine = pl.ds(pl.multiple_of(n * 8, 8), 8)
                for k in range(2):
                    block = 2 * core + k
                    out_ref[n, :, 1024 + k * 512 : 1536 + k * 512] = (
                        gw_ref[block, mine, :] + gw_before[block, mine, :]
                    ).astype(BF16)
        chunk_copy(out_ref, out_any, out_sems, c).start()
        return carry

    lax.fori_loop(0, CHUNKS, empty, 0)
    for c in range(CHUNKS):
        stores.append(chunk_copy(out_ref, out_any, out_sems, c))
    for store in stores:
        store.wait()


def window_pass(core, x, gain, shift, w_qkv, w_out, bias, mask, sums):
    last = sums is not None
    windows = x.shape[1] // 2
    cells = windows * CELLS
    shape = jax.ShapeDtypeStruct
    hbm = pl.BlockSpec(memory_space=pltpu.HBM)
    vmem = pl.BlockSpec(memory_space=pltpu.VMEM)
    grads = shape((4, 512, 512), F32)
    ln = shape((2, 8, 512), F32)
    if last:
        outs = [shape((CELLS, 8, 2048), BF16), shape((512, 1024), BF16), shape((8, 128), F32)]
    else:
        outs = [shape((CELLS, windows, 512), BF16), grads, ln]

    def kernel(*refs):
        window_kernel(*refs, last=last)

    return pl.pallas_call(
        kernel,
        in_specs=[
            pl.BlockSpec(memory_space=pltpu.SMEM),
            hbm, vmem, vmem, vmem, vmem, vmem, vmem,
        ]
        + ([hbm, vmem] if last else []),
        out_specs=[hbm, hbm, vmem],
        out_shape=outs,
        scratch_shapes=[
            pltpu.VMEM(x.shape, BF16),
            pltpu.VMEM(grads.shape, F32),
            pltpu.VMEM(outs[0].shape, BF16),
            pltpu.VMEM((4, cells + windows, 128), F32),
            pltpu.VMEM((4, cells + windows, 128), F32),
            pltpu.VMEM((ROWS, 1536), BF16),
            pltpu.VMEM((ROWS, 512), BF16),
            pltpu.VMEM((ROWS, 1536), BF16),
            pltpu.VMEM((ROWS, 512), BF16),
            pltpu.SemaphoreType.DMA((CHUNKS,)),
            pltpu.SemaphoreType.DMA((4,)),
            pltpu.SemaphoreType.DMA((CHUNKS,)),
        ]
        + (
            [
                pltpu.VMEM((512, 1024), BF16),
                pltpu.VMEM(grads.shape, F32),
                pltpu.VMEM(ln.shape, F32),
            ]
            if last
            else []
        ),
        compiler_params=pltpu.CompilerParams(vmem_limit_bytes=KERNEL_MIB * MIB),
        cost_estimate=pl.CostEstimate(
            flops=20 * 10**9, bytes_accessed=12 * MIB, transcendentals=10**6
        ),
        name="window_last" if last else "window_first",
    )(core, x, gain, shift, w_qkv, w_out, bias, mask, *(sums or ()))


def stage(*arrays):
    def kernel(*refs):
        count = len(arrays)
        sems = refs[-1]
        copies = [
            pltpu.make_async_copy(refs[i], refs[count + i], sems.at[i]) for i in range(count)
        ]
        for copy in copies:
            copy.start()
        for copy in copies:
            copy.wait()

    return pl.pallas_call(
        kernel,
        in_specs=[pl.BlockSpec(memory_space=pltpu.HBM)] * len(arrays),
        out_specs=[pl.BlockSpec(memory_space=pltpu.VMEM)] * len(arrays),
        out_shape=[jax.ShapeDtypeStruct(a.shape, a.dtype) for a in arrays],
        scratch_shapes=[pltpu.SemaphoreType.DMA((len(arrays),))],
        compiler_params=pltpu.CompilerParams(vmem_limit_bytes=KERNEL_MIB * MIB),
        cost_estimate=pl.CostEstimate(flops=0, bytes_accessed=3 * MIB, transcendentals=0),
        name="stage_constants",
    )(*arrays)


def pack(latent, cotangent, part, half):
    peers, _, width = latent.shape
    pieces = 4
    size = peers // pieces

    def kernel(latent_any, cotangent_any, out_any, held, in_sems, out_sems):
        def load(c, k):
            block = pl.ds(c * size, size)
            source = (latent_any, cotangent_any)[k]
            return pltpu.make_async_copy(
                source.at[block, pl.ds(part * half, half)],
                held.at[block, pl.ds(k * half, half)],
                in_sems.at[2 * c + k],
            )

        def store(c):
            block = pl.ds(c * size, size)
            return pltpu.make_async_copy(held.at[block], out_any.at[block], out_sems.at[c])

        for c in range(pieces):
            load(c, 0).start()
            load(c, 1).start()
        for c in range(pieces):
            load(c, 0).wait()
            load(c, 1).wait()
            store(c).start()
        for c in range(pieces):
            store(c).wait()

    hbm = pl.BlockSpec(memory_space=pltpu.HBM)
    return pl.pallas_call(
        kernel,
        in_specs=[hbm, hbm],
        out_specs=hbm,
        out_shape=jax.ShapeDtypeStruct((peers, 2 * half, width), BF16),
        scratch_shapes=[
            pltpu.VMEM((peers, 2 * half, width), BF16),
            pltpu.SemaphoreType.DMA((2 * pieces,)),
            pltpu.SemaphoreType.DMA((pieces,)),
        ],
        compiler_params=pltpu.CompilerParams(vmem_limit_bytes=VMEM_MIB * MIB),
        cost_estimate=pl.CostEstimate(flops=0, bytes_accessed=4 * MIB, transcendentals=0),
        name="pack_part",
    )(latent, cotangent)


def place_kernel(core_ref, half_ref, *refs, own):
    gq_any, go_any, wide, sems = refs[-4:]
    low = core_ref[0] == (0 if own else 1)
    pieces = 4
    size = wide.shape[0] // pieces

    def copies(p):
        rows = pl.ds(p * size, size)
        first = pltpu.make_async_copy(
            wide.at[rows], gq_any.at[rows, pl.ds(0, 1024)], sems.at[p]
        )
        second = pltpu.make_async_copy(
            wide.at[rows, pl.ds(0, 512)], gq_any.at[rows, pl.ds(1024, 512)], sems.at[p]
        )
        third = pltpu.make_async_copy(
            wide.at[rows, pl.ds(512, 512)], go_any.at[rows], sems.at[pieces + p]
        )
        return first, second, third

    for p in range(pieces):
        rows = pl.ds(p * size, size)
        wide[rows, :] = half_ref[rows, :1024].astype(F32)

        @pl.when(low)
        def _():
            copies(p)[0].start()

        @pl.when(jnp.logical_not(low))
        def _():
            copies(p)[1].start()
            copies(p)[2].start()

    for p in range(pieces):

        @pl.when(low)
        def _():
            copies(p)[0].wait()

        @pl.when(jnp.logical_not(low))
        def _():
            copies(p)[1].wait()
            copies(p)[2].wait()


def place(core, half, placed):
    own = placed is None
    hbm = pl.BlockSpec(memory_space=pltpu.HBM)

    def kernel(*refs):
        place_kernel(*refs, own=own)

    return pl.pallas_call(
        kernel,
        in_specs=[
            pl.BlockSpec(memory_space=pltpu.SMEM),
            pl.BlockSpec(memory_space=pltpu.VMEM),
        ]
        + ([] if own else [hbm, hbm]),
        out_specs=[hbm, hbm],
        out_shape=[
            jax.ShapeDtypeStruct((512, 1536), F32),
            jax.ShapeDtypeStruct((512, 512), F32),
        ],
        scratch_shapes=[pltpu.VMEM((512, 1024), F32), pltpu.SemaphoreType.DMA((8,))],
        input_output_aliases={} if own else {2: 0, 3: 1},
        compiler_params=pltpu.CompilerParams(vmem_limit_bytes=16 * MIB),
        cost_estimate=pl.CostEstimate(flops=0, bytes_accessed=3 * MIB, transcendentals=0),
        name="place_own" if own else "place_other",
    )(core, half, *(placed or ()))


def bias_tables(rel_bias):
    position = jnp.arange(CELLS, dtype=jnp.int32)
    prow = position // 8
    pcol = position % 8
    offset = (prow[None, :] - prow[:, None] + 7) * 15 + (pcol[None, :] - pcol[:, None] + 7)
    onehot = (offset.reshape(1, -1) == jnp.arange(225, dtype=jnp.int32)[:, None]).astype(F32)
    full = jnp.dot(rel_bias, onehot, precision=lax.Precision.HIGHEST)
    full = full.reshape(GROUPS, HEADS // GROUPS, CELLS, CELLS).transpose(0, 2, 1, 3)
    return full.reshape(GROUPS, CELLS, 256)


def after(value, *others):
    return lax.optimization_barrier((value,) + others)[0]


def exchange(array):
    return lax.all_to_all(array, ("gx", "gh"), split_axis=0, concat_axis=0, tiled=True)


def swap_cores(array):
    return lax.ppermute(array, "core", [(0, 1), (1, 0)])


def body(latent, cotangent, gain, shift, w_qkv, w_out, rel_bias):
    rows, cols, width = latent.shape
    peers = lax.axis_size("gx") * lax.axis_size("gh")
    windows = rows * cols // peers
    half = windows // PARTS
    norm = 1.0 / math.sqrt(rows * cols * peers * lax.axis_size("core"))
    core = lax.axis_index("core")
    gain = gain.reshape(1, width)
    shift = shift.reshape(1, width)
    lane = jnp.arange(128, dtype=jnp.int32) // 32
    mask = jnp.broadcast_to(
        (lane[None, None, :] == jnp.arange(4, dtype=jnp.int32)[:, None, None]).astype(BF16),
        (4, CELLS, 128),
    )
    bias = bias_tables(rel_bias)
    w_qkv, w_out, bias, mask = stage(w_qkv, w_out, bias, mask)
    consts = (gain, shift, w_qkv, w_out, bias, mask)
    core_id = core.astype(jnp.int32).reshape(1)

    latent = latent.reshape(peers, windows, width)
    cotangent = cotangent.reshape(peers, windows, width)
    x_first = exchange(pack(latent, cotangent, 0, half))
    x_second = exchange(after(pack(latent, cotangent, 1, half), x_first))
    d_first, gw, ln = window_pass(core_id, x_first, *consts, None)
    back_first = exchange(d_first)
    payload, other, ln = window_pass(core_id, x_second, *consts, (gw, ln))

    other, ln = lax.optimization_barrier((other, ln, back_first))[:2]
    received = swap_cores(other).reshape(peers, 8, 1024)
    ln = ln + swap_cores(ln)
    mine = payload[:, :, 1024:].astype(F32) + received.astype(F32)
    moved = exchange(payload.at[:, :, 1024:].set(mine.astype(BF16)))
    total = jnp.sum(moved[:, :, 1024:].astype(F32), axis=0) * norm
    share = jnp.concatenate([total, ln], axis=1).astype(BF16)
    full = exchange(jnp.broadcast_to(share[None], (peers, 8, 1152)))
    result = jnp.concatenate(
        [back_first, moved[:, :, :width], moved[:, :, width : 2 * width]], axis=1
    )
    full, result = lax.optimization_barrier((full, result))
    ours = full.reshape(width, 1152)
    theirs = swap_cores(ours)
    placed = place(core_id, ours, None)
    grad_qkv, grad_out = place(core_id, theirs, placed)
    ln_total = (jnp.sum(full[:, :, 1024:].astype(F32), axis=0) * norm).reshape(2, width)
    return (result.reshape(rows, cols, width), grad_qkv, grad_out, ln_total[0], ln_total[1])


def solution(mesh):
    cores = mesh.devices.reshape(mesh.shape["gx"], mesh.shape["gy"] // 2, 2)
    inner = Mesh(cores, ("gx", "gh", "core"))
    block = P("gx", ("gh", "core"), None)
    return jax.shard_map(
        body,
        mesh=inner,
        in_specs=(block, block, P(), P(), P(), P(), P()),
        out_specs=(block, P(), P(), P(), P()),
        check_vma=False,
    )
```
